256 devices in a mesh: section: 8 (over z_lo, x), row: 32 (over z_hi, y, core).
Axes of the slice: x: 4, y: 4, z: 8 (z_hi: 4, z_lo: 2; z = z_hi * 2 + z_lo), core: 2. Of those that a mesh axis runs over, the one named last changes fastest.
Arguments:
- sections: float32 [8, 4096, 4096], P('section', None, 'row'), may hold values from -18 to 18
- preceding: float32 [4096, 4096], P(None, 'row'), may hold values from -18 to 18
Outputs:
- surface: float32 [8, 4096, 4096], P('section', None, 'row')
- peaks: float32 [8], P('section')
The draws below stay inside these ranges and needn't reach their ends.
All inputs are finite; a program needn't handle non-finite values.
Results may differ from the reference program's by a relative error of at most 0.0003.
Values sent between devices are 32-bit elements; how exact they have to be, the bound alone decides.
A program may use at most 128 MiB of HBM per device.

```python
import jax
import jax.numpy as jnp
from jax import lax

NX = 4096
NY = 4096
SECT = 8


def shared_base(key):
    return jax.random.truncated_normal(key, -5.0, 5.0, (NX, NY), jnp.float32)


def noisy_field(key, count):
    key_noise = jax.random.fold_in(key, 0)
    return jax.random.truncated_normal(key_noise, -5.0, 5.0, (count, NX, NY), jnp.float32)


def draw_sections(key, part):
    base = shared_base(key)
    key = jax.random.fold_in(key, 11)
    key_noise, key_sx, key_sy = jax.random.split(key, 3)
    shift_x = jax.random.randint(key_sx, (SECT,), 0, NX)
    shift_y = jax.random.randint(key_sy, (SECT,), 0, NY)
    moved = jax.vmap(lambda first, second: jnp.roll(jnp.roll(base, first, 0), second, 1))(shift_x, shift_y)
    return 0.06 * moved + noisy_field(key_noise, SECT)


def draw_preceding(key, part):
    base = shared_base(key)
    key = jax.random.fold_in(key, 12)
    key_noise, key_sx, key_sy = jax.random.split(key, 3)
    shift_x = jax.random.randint(key_sx, (), 0, NX)
    shift_y = jax.random.randint(key_sy, (), 0, NY)
    moved = jnp.roll(jnp.roll(base, shift_x, 0), shift_y, 1)
    return 0.06 * moved + noisy_field(key_noise, 1)[0]


def setup_inputs(seed: int = 0) -> dict:
    splits = jax.random.split(jax.random.key(seed), 3)
    sections = draw_sections(jax.random.fold_in(splits[2], 71), 0)
    preceding = draw_preceding(jax.random.fold_in(splits[2], 71), 0)
    return dict(sections=sections, preceding=preceding)


floor_share = 0.02


def reference(sections, preceding):
    prior_spec = jnp.fft.fft2(preceding)

    def step(carry, pixels):
        current = jnp.fft.fft2(pixels)
        cross = carry * jnp.conj(current)
        magnitude = jnp.abs(carry) * jnp.abs(current)
        ratio = cross / jnp.maximum(magnitude, floor_share * NX * NY)
        result = jnp.real(jnp.fft.ifft2(ratio)) * NY
        return current, (result, jnp.max(result))

    last, outputs = lax.scan(step, prior_spec, sections)
    return outputs[0], outputs[1]
```

```python
import functools
import math

import jax
import jax.numpy as jnp
import ml_dtypes
import numpy as np
from jax import lax
from jax.experimental import pallas as pl
from jax.experimental.pallas import tpu as pltpu
from jax.sharding import PartitionSpec as P

MESH = pl.DeviceIdType.MESH
F32 = jnp.float32
BF16 = jnp.bfloat16

N = 4096
R = 32
L = 128
SEC = 8
ROW = 32
DEV = SEC * ROW
UNITS = 16
FLOOR = 0.02 * 4096 * 4096
VMEM_LIMIT = 48 << 20


def split(table):
    high = table.astype(ml_dtypes.bfloat16)
    low = (table - high.astype(np.float64)).astype(ml_dtypes.bfloat16)
    return np.stack([high, low], -3)


@functools.lru_cache(None)
def tables():
    n2 = np.arange(L)
    row = np.arange(L)
    fwd = np.zeros((UNITS, 16, 2, 8, 2, L))
    inv = np.zeros((UNITS, 2, L, 16, 2, 8))

    def angles(kx):
        turn = 2 * np.pi / N * (np.outer(kx, n2) % N)
        return np.cos(turn).reshape(-1, 8, L), np.sin(turn).reshape(-1, 8, L)

    for u in range(1, UNITS):
        c, s = angles(u + R * row)
        fwd[u, :, 0, :, 0], fwd[u, :, 0, :, 1] = c, s
        fwd[u, :, 1, :, 0], fwd[u, :, 1, :, 1] = -s, c
        ct, st = np.moveaxis(c, 2, 0), np.moveaxis(s, 2, 0)
        inv[u, 0, :, :, 0], inv[u, 0, :, :, 1] = ct, -st
        inv[u, 1, :, :, 0], inv[u, 1, :, :, 1] = st, ct
    for half, base in ((0, 0), (1, 16)):
        c, s = angles(base + R * np.arange(L // 2))
        js = slice(8 * half, 8 * half + 8)
        ti, tr = -s, c
        bi, br = -2 * s, 2 * c
        if half == 0:
            ti[0, 0] = (-1.0) ** n2
            bi[0, 0] = (-1.0) ** n2
            br[0, 0] = 1.0
        fwd[0, js, 0, :, half], fwd[0, js, 1, :, half] = tr, ti
        inv[0, half, :, js, 0] = np.moveaxis(br, 2, 0)
        inv[0, half, :, js, 1] = np.moveaxis(bi, 2, 0)
    fwd = split(fwd.reshape(UNITS, 2 * L, 2 * L))
    inv = split(inv.reshape(UNITS, 2 * L, 2 * L) / N)
    turn = 2 * np.pi / L * (np.outer(row, row) % L)
    c, s = np.cos(turn), np.sin(turn)
    lanes = split(np.block([[c, -s], [s, c]]))
    lanes_inv = split(np.block([[c, s], [-s, c]]))
    turn = 2 * np.pi / N * np.outer(np.arange(R + 1), row)
    twist = np.stack([np.cos(turn), np.sin(turn)], 1).astype(np.float32)
    twist = np.broadcast_to(twist[:, :, None, :], (R + 1, 2, 8, L)).copy()
    return fwd, inv, lanes, lanes_inv, twist


def turned(z, k, n, sign):
    k %= n
    re, im = z
    if k == 0:
        return z
    if 4 * k == n:
        return (-im, re) if sign > 0 else (im, -re)
    if 2 * k == n:
        return (-re, -im)
    if 8 * k == n:
        h = math.sqrt(0.5)
        return ((re - im) * h, (re + im) * h) if sign > 0 else ((re + im) * h, (im - re) * h)
    c, s = math.cos(2 * math.pi * k / n), sign * math.sin(2 * math.pi * k / n)
    return (re * c - im * s, re * s + im * c)


def add(a, b):
    return (a[0] + b[0], a[1] + b[1])


def sub(a, b):
    return (a[0] - b[0], a[1] - b[1])


def complex_dft(z, sign):
    n = len(z)
    if n == 1:
        return z
    even, odd = complex_dft(z[0::2], sign), complex_dft(z[1::2], sign)
    out = [None] * n
    for k in range(n // 2):
        t = turned(odd[k], k, n, sign)
        out[k], out[k + n // 2] = add(even[k], t), sub(even[k], t)
    return out


def real_dft(x):
    n = len(x)
    if n == 2:
        return [(x[0] + x[1], None), (x[0] - x[1], None)]
    even, odd = real_dft(x[0::2]), real_dft(x[1::2])
    out = [None] * (n // 2 + 1)
    out[0] = (even[0][0] + odd[0][0], None)
    out[n // 2] = (even[0][0] - odd[0][0], None)
    for k in range(1, n // 4):
        t = turned(odd[k], k, n, -1)
        out[k] = add(even[k], t)
        d = sub(even[k], t)
        out[n // 2 - k] = (d[0], -d[1])
    out[n // 4] = (even[n // 4][0], -odd[n // 4][0])
    return out


def real_dft_back(z):
    n = 2 * (len(z) - 1)
    if n == 2:
        return [z[0][0] + z[1][0], z[0][0] - z[1][0]]
    even, odd = [None] * (n // 4 + 1), [None] * (n // 4 + 1)
    even[0] = (z[0][0] + z[n // 2][0], None)
    odd[0] = (z[0][0] - z[n // 2][0], None)
    for k in range(1, n // 4):
        mirror = (z[n // 2 - k][0], -z[n // 2 - k][1])
        even[k] = add(z[k], mirror)
        odd[k] = turned(sub(z[k], mirror), k, n, 1)
    even[n // 4] = (z[n // 4][0] * 2.0, None)
    odd[n // 4] = (z[n // 4][1] * -2.0, None)
    out = [None] * n
    out[0::2], out[1::2] = real_dft_back(even), real_dft_back(odd)
    return out


def parts(value):
    high = value.astype(BF16)
    return high, (value - high.astype(F32)).astype(BF16)


def dot(a, b):
    return jnp.dot(a, b, preferred_element_type=F32)


def table_times(table_ref, value):
    high, low = parts(value)
    both = dot(table_ref[0], jnp.concatenate([high, low], 1))
    width = value.shape[1]
    return both[:, :width] + both[:, width:] + dot(table_ref[1], high)


def times_table(value, table_ref):
    high, low = parts(value)
    return dot(high, table_ref[0]) + dot(low, table_ref[0]) + dot(high, table_ref[1])


def x_first(pixels_ref, a_ref):
    @pl.loop(0, L // 8)
    def _(g):
        rows = pl.ds(pl.multiple_of(g * 8, 8), 8)
        more = pl.ds(pl.multiple_of(g * 8 + L, 8), 8)
        out = real_dft([pixels_ref[n, rows, :] for n in range(R)])
        a_ref[0, rows, :] = out[0][0]
        a_ref[0, more, :] = out[R // 2][0]
        for u in range(1, UNITS):
            a_ref[u, rows, :] = out[u][0]
            a_ref[u, more, :] = out[u][1]


def x_unit(table_ref, value):
    return table_times(table_ref, value).reshape(16, 2, 8, L)


def x_last(b_ref, out_ref):
    def body(g, top):
        rows = pl.ds(pl.multiple_of(g * 8, 8), 8)
        more = pl.ds(pl.multiple_of(g * 8 + L, 8), 8)
        z = [(b_ref[0, rows, :], None)]
        z += [(b_ref[u, rows, :], b_ref[u, more, :]) for u in range(1, UNITS)]
        z += [(b_ref[0, more, :], None)]
        out = real_dft_back(z)
        for n in range(R):
            out_ref[n, rows, :] = out[n]
        while len(out) > 1:
            out = [jnp.maximum(a, b) for a, b in zip(out[0::2], out[1::2])]
        return jnp.maximum(top, out[0])

    return lax.fori_loop(0, L // 8, body, jnp.full((8, L), -jnp.inf, F32))


def y_forward(tile_ref, twist_ref, lanes_ref, v_ref, own_ref, mirror_ref, special):
    z = complex_dft([(tile_ref[p, 0], tile_ref[p, 1]) for p in range(R)], -1)
    for a in range(R):
        re, im = z[a]
        if a:
            c, s = twist_ref[a, 0], twist_ref[a, 1]
            re, im = re * c + im * s, im * c - re * s
        v_ref[a, :, :L] = re
        v_ref[a, :, L:] = im
    own_ref[...] = times_table(v_ref[...].reshape(R * 8, 2 * L), lanes_ref).reshape(R, 8, 2 * L)

    @pl.when(special)
    def _():
        c, s = twist_ref[R, 0], twist_ref[R, 1]

        @pl.loop(0, R)
        def _(a):
            first = a == 0
            back = lax.rem(R - a, R)
            re, im = v_ref[back, :, :L], -v_ref[back, :, L:]
            mirror_ref[a, :, :L] = jnp.where(first, re, re * c + im * s)
            mirror_ref[a, :, L:] = jnp.where(first, im, im * c - re * s)

        value = mirror_ref[...].reshape(R * 8, 2 * L)
        mirror_ref[...] = times_table(value, lanes_ref).reshape(R, 8, 2 * L)


def phase(pr, pi, our, oi):
    re = pr * our + pi * oi
    im = pi * our - pr * oi
    scale = lax.rsqrt(jnp.maximum(re * re + im * im, FLOOR * FLOOR))
    return re * scale, im * scale


def y_ratio(prior_ref, own_ref, prior_mirror_ref, own_mirror_ref, v_ref, special):
    re, im = phase(prior_ref[:, :, :L], prior_ref[:, :, L:], own_ref[:, :, :L], own_ref[:, :, L:])
    v_ref[:, :, :L] = re
    v_ref[:, :, L:] = im

    @pl.when(special)
    def _():
        def both(ref, mirror, a):
            re, im, mre, mim = ref[a, :, :L], ref[a, :, L:], mirror[a, :, :L], mirror[a, :, L:]
            low = ((re + mre) * 0.5, (im + mim) * 0.5)
            high = ((im - mim) * 0.5, (mre - re) * 0.5)
            return low, high

        packed = lax.broadcasted_iota(jnp.int32, (8, L), 0) == 0

        @pl.loop(0, R)
        def _(a):
            prior_low, prior_high = both(prior_ref, prior_mirror_ref, a)
            own_low, own_high = both(own_ref, own_mirror_ref, a)
            low = phase(*prior_low, *own_low)
            high = phase(*prior_high, *own_high)
            v_ref[a, :, :L] = jnp.where(packed, low[0] - high[1], v_ref[a, :, :L])
            v_ref[a, :, L:] = jnp.where(packed, low[1] + high[0], v_ref[a, :, L:])


def y_back(v_ref, twist_ref, lanes_inv_ref, out_ref):
    v_ref[...] = times_table(v_ref[...].reshape(R * 8, 2 * L), lanes_inv_ref).reshape(R, 8, 2 * L)
    z = []
    for a in range(R):
        re, im = v_ref[a, :, :L], v_ref[a, :, L:]
        if a:
            c, s = twist_ref[a, 0], twist_ref[a, 1]
            re, im = re * c - im * s, im * c + re * s
        z.append((re, im))
    z = complex_dft(z, 1)
    for p in range(R):
        out_ref[p, 0] = z[p][0]
        out_ref[p, 1] = z[p][1]


def forward_kernel(sec_ref, pre_ref, fwd_ref, x_ref, xp_ref, a_ref):
    s = lax.axis_index("section")
    x_first(pre_ref, a_ref)
    for h in range(2):
        u = 2 * s + h
        xp_ref[pl.ds(h * 16, 16)] = x_unit(fwd_ref.at[u], a_ref[u])
    x_first(sec_ref, a_ref)

    @pl.loop(0, UNITS)
    def _(u):
        x_ref[pl.ds(u * 16, 16)] = x_unit(fwd_ref.at[u], a_ref[u])


def middle_kernel(r_ref, rp_ref, lanes_ref, lanes_inv_ref, twist_ref, y_ref, v_ref, spec_ref, mirror_ref):
    special = (lax.axis_index("section") == 0) & (lax.axis_index("row") == 0)
    y_forward(rp_ref, twist_ref, lanes_ref, v_ref, spec_ref.at[1], mirror_ref.at[1], special)

    @pl.loop(0, SEC)
    def _(s):
        own, prior = lax.rem(s, 2), lax.rem(s + 1, 2)
        y_forward(r_ref.at[s], twist_ref, lanes_ref, v_ref, spec_ref.at[own], mirror_ref.at[own], special)
        y_ratio(spec_ref.at[prior], spec_ref.at[own], mirror_ref.at[prior], mirror_ref.at[own], v_ref, special)
        y_back(v_ref, twist_ref, lanes_inv_ref, y_ref.at[s])


def back_kernel(q_ref, inv_ref, out_ref, top_ref, b_ref):
    @pl.loop(0, UNITS)
    def _(u):
        value = q_ref[pl.ds(u * 16, 16)].reshape(2 * L, L)
        b_ref[u] = table_times(inv_ref.at[u], value)

    top_ref[...] = x_last(b_ref, out_ref)


def here():
    return lax.axis_index("section"), lax.axis_index("row")


def exchange_kernel(with_first, *refs):
    if with_first:
        x_ref, xp_ref, o_ref, op_ref, send_sem, recv_sem, loc_sem = refs
    else:
        x_ref, o_ref, send_sem, recv_sem, loc_sem = refs
    s, p = here()
    bar = pltpu.get_barrier_semaphore()

    @pl.loop(1, DEV)
    def _(i):
        to = ((s + i // ROW) % SEC, (p + i % ROW) % ROW)
        pl.semaphore_signal(bar, inc=1, device_id=to, device_id_type=MESH)

    pl.semaphore_wait(bar, DEV - 1)
    me = s * ROW + p
    own = [pltpu.make_async_copy(x_ref.at[me], o_ref.at[me], loc_sem.at[0])]
    if with_first:
        own.append(pltpu.make_async_copy(xp_ref.at[p], op_ref.at[p], loc_sem.at[1]))
    for copy in own:
        copy.start()
    if with_first:

        @pl.loop(1, ROW)
        def _(i):
            to = (p + i) % ROW
            pltpu.make_async_remote_copy(
                xp_ref.at[to], op_ref.at[p], send_sem.at[1], recv_sem.at[1], device_id=(s, to), device_id_type=MESH
            ).start()

    @pl.loop(1, DEV)
    def _(i):
        ts, tp = (s + i // ROW) % SEC, (p + i % ROW) % ROW
        pltpu.make_async_remote_copy(
            x_ref.at[ts * ROW + tp], o_ref.at[me], send_sem.at[0], recv_sem.at[0], device_id=(ts, tp), device_id_type=MESH
        ).start()

    for copy in own:
        copy.wait()
    for sem in (recv_sem, send_sem):
        count = pl.ds(0, DEV - 1)
        pltpu.make_async_copy(x_ref.at[count], o_ref.at[count], sem.at[0]).wait()
        if with_first:
            count = pl.ds(0, ROW - 1)
            pltpu.make_async_copy(xp_ref.at[count], op_ref.at[count], sem.at[1]).wait()


def peak_kernel(top_ref, peak_ref, mine_ref, all_ref, send_sem, recv_sem):
    s, p = here()
    bar = pltpu.get_barrier_semaphore()

    @pl.loop(1, ROW)
    def _(i):
        pl.semaphore_signal(bar, inc=1, device_id=(s, (p + i) % ROW), device_id_type=MESH)

    pl.semaphore_wait(bar, ROW - 1)
    mine_ref[...] = top_ref[...]
    all_ref[p] = top_ref[...]

    @pl.loop(1, ROW)
    def _(i):
        pltpu.make_async_remote_copy(
            mine_ref, all_ref.at[p], send_sem, recv_sem, device_id=(s, (p + i) % ROW), device_id_type=MESH
        ).start()

    count = pl.ds(0, ROW - 1)
    for sem in (recv_sem, send_sem):
        pltpu.make_async_copy(all_ref.at[count], all_ref.at[count], sem).wait()
    peak_ref[...] = jnp.max(all_ref[...], axis=0)


VMEM = pl.BlockSpec(memory_space=pltpu.VMEM)
ANY = pl.BlockSpec(memory_space=pl.ANY)


def f32(*shape):
    return jax.ShapeDtypeStruct(shape, F32)


def call(kernel, args, outs, scratch, place=VMEM, collective=None):
    extra = {} if collective is None else dict(collective_id=collective, has_side_effects=True)
    return pl.pallas_call(
        kernel,
        out_shape=outs,
        in_specs=[place] * len(args),
        out_specs=jax.tree.map(lambda _: place, outs),
        scratch_shapes=scratch,
        compiler_params=pltpu.CompilerParams(vmem_limit_bytes=VMEM_LIMIT, **extra),
    )(*args)


def local(sections, preceding):
    fwd, inv, lanes, lanes_inv, twist = (jnp.asarray(t) for t in tables())
    block = (2, 8, L)
    sem = pltpu.SemaphoreType.DMA
    x, xp = call(
        forward_kernel,
        (sections.reshape(R, L, L), preceding.reshape(R, L, L), fwd),
        (f32(DEV, *block), f32(ROW, *block)),
        [pltpu.VMEM((UNITS, 2 * L, L), F32)],
    )
    r, rp = call(
        functools.partial(exchange_kernel, True), (x, xp), (f32(DEV, *block), f32(ROW, *block)), [sem((2,))] * 3, ANY, 1
    )
    y = call(
        middle_kernel,
        (r.reshape(SEC, ROW, *block), rp, lanes, lanes_inv, twist),
        f32(SEC, ROW, *block),
        [pltpu.VMEM((R, 8, 2 * L), F32)] + [pltpu.VMEM((2, R, 8, 2 * L), F32)] * 2,
    )
    q = call(functools.partial(exchange_kernel, False), (y.reshape(DEV, *block),), f32(DEV, *block), [sem((2,))] * 3, ANY, 2)
    surface, top = call(
        back_kernel, (q, inv), (f32(R, L, L), f32(8, L)), [pltpu.VMEM((UNITS, 2 * L, L), F32)]
    )
    peak = call(
        peak_kernel, (top,), f32(8, L), [pltpu.VMEM((8, L), F32), pltpu.VMEM((ROW, 8, L), F32), sem, sem], VMEM, 3
    )
    return surface.reshape(1, N, L), jnp.max(peak).reshape(1)


def solution(mesh):
    in_specs = (P("section", None, "row"), P(None, "row"))
    out_specs = (P("section", None, "row"), P("section"))
    return jax.shard_map(local, mesh=mesh, in_specs=in_specs, out_specs=out_specs, check_vma=False)
```

```python
import functools
import math

import jax
import jax.numpy as jnp
import ml_dtypes
import numpy as np
from jax import lax
from jax.experimental import pallas as pl
from jax.experimental.pallas import tpu as pltpu
from jax.sharding import PartitionSpec as P

MESH = pl.DeviceIdType.MESH
F32 = jnp.float32
BF16 = jnp.bfloat16

N = 4096
R = 32
L = 128
SEC = 8
ROW = 32
DEV = SEC * ROW
UNITS = 16
FLOOR = 0.02 * 4096 * 4096
VMEM_LIMIT = 48 << 20


def split(table):
    high = table.astype(ml_dtypes.bfloat16)
    low = (table - high.astype(np.float64)).astype(ml_dtypes.bfloat16)
    return np.stack([high, low], -3)


@functools.lru_cache(None)
def tables():
    n2 = np.arange(L)
    row = np.arange(L)
    fwd = np.zeros((UNITS, 16, 2, 8, 2, L))
    inv = np.zeros((UNITS, 2, L, 16, 2, 8))

    def angles(kx):
        turn = 2 * np.pi / N * (np.outer(kx, n2) % N)
        return np.cos(turn).reshape(-1, 8, L), np.sin(turn).reshape(-1, 8, L)

    for u in range(1, UNITS):
        c, s = angles(u + R * row)
        fwd[u, :, 0, :, 0], fwd[u, :, 0, :, 1] = c, s
        fwd[u, :, 1, :, 0], fwd[u, :, 1, :, 1] = -s, c
        ct, st = np.moveaxis(c, 2, 0), np.moveaxis(s, 2, 0)
        inv[u, 0, :, :, 0], inv[u, 0, :, :, 1] = ct, -st
        inv[u, 1, :, :, 0], inv[u, 1, :, :, 1] = st, ct
    for half, base in ((0, 0), (1, 16)):
        c, s = angles(base + R * np.arange(L // 2))
        js = slice(8 * half, 8 * half + 8)
        ti, tr = -s, c
        bi, br = -2 * s, 2 * c
        if half == 0:
            ti[0, 0] = (-1.0) ** n2
            bi[0, 0] = (-1.0) ** n2
            br[0, 0] = 1.0
        fwd[0, js, 0, :, half], fwd[0, js, 1, :, half] = tr, ti
        inv[0, half, :, js, 0] = np.moveaxis(br, 2, 0)
        inv[0, half, :, js, 1] = np.moveaxis(bi, 2, 0)
    fwd = split(fwd.reshape(UNITS, 2 * L, 2 * L))
    inv = split(inv.reshape(UNITS, 2 * L, 2 * L) / N)
    turn = 2 * np.pi / L * (np.outer(row, row) % L)
    c, s = np.cos(turn), np.sin(turn)
    lanes = split(np.block([[c, -s], [s, c]]))
    lanes_inv = split(np.block([[c, s], [-s, c]]))
    turn = 2 * np.pi / N * np.outer(np.arange(R + 1), row)
    twist = np.stack([np.cos(turn), np.sin(turn)], 1).astype(np.float32)
    twist = np.broadcast_to(twist[:, :, None, :], (R + 1, 2, 8, L)).copy()
    return fwd, inv, lanes, lanes_inv, twist


def turned(z, k, n, sign):
    k %= n
    re, im = z
    if k == 0:
        return z
    if 4 * k == n:
        return (-im, re) if sign > 0 else (im, -re)
    if 2 * k == n:
        return (-re, -im)
    if 8 * k == n:
        h = math.sqrt(0.5)
        return ((re - im) * h, (re + im) * h) if sign > 0 else ((re + im) * h, (im - re) * h)
    c, s = math.cos(2 * math.pi * k / n), sign * math.sin(2 * math.pi * k / n)
    return (re * c - im * s, re * s + im * c)


def add(a, b):
    return (a[0] + b[0], a[1] + b[1])


def sub(a, b):
    return (a[0] - b[0], a[1] - b[1])


def complex_dft(z, sign):
    n = len(z)
    if n == 1:
        return z
    even, odd = complex_dft(z[0::2], sign), complex_dft(z[1::2], sign)
    out = [None] * n
    for k in range(n // 2):
        t = turned(odd[k], k, n, sign)
        out[k], out[k + n // 2] = add(even[k], t), sub(even[k], t)
    return out


def real_dft(x):
    n = len(x)
    if n == 2:
        return [(x[0] + x[1], None), (x[0] - x[1], None)]
    even, odd = real_dft(x[0::2]), real_dft(x[1::2])
    out = [None] * (n // 2 + 1)
    out[0] = (even[0][0] + odd[0][0], None)
    out[n // 2] = (even[0][0] - odd[0][0], None)
    for k in range(1, n // 4):
        t = turned(odd[k], k, n, -1)
        out[k] = add(even[k], t)
        d = sub(even[k], t)
        out[n // 2 - k] = (d[0], -d[1])
    out[n // 4] = (even[n // 4][0], -odd[n // 4][0])
    return out


def real_dft_back(z):
    n = 2 * (len(z) - 1)
    if n == 2:
        return [z[0][0] + z[1][0], z[0][0] - z[1][0]]
    even, odd = [None] * (n // 4 + 1), [None] * (n // 4 + 1)
    even[0] = (z[0][0] + z[n // 2][0], None)
    odd[0] = (z[0][0] - z[n // 2][0], None)
    for k in range(1, n // 4):
        mirror = (z[n // 2 - k][0], -z[n // 2 - k][1])
        even[k] = add(z[k], mirror)
        odd[k] = turned(sub(z[k], mirror), k, n, 1)
    even[n // 4] = (z[n // 4][0] * 2.0, None)
    odd[n // 4] = (z[n // 4][1] * -2.0, None)
    out = [None] * n
    out[0::2], out[1::2] = real_dft_back(even), real_dft_back(odd)
    return out


def parts(value):
    high = value.astype(BF16)
    return high, (value - high.astype(F32)).astype(BF16)


def dot(a, b):
    return jnp.dot(a, b, preferred_element_type=F32)


def table_times(table_ref, value):
    high, low = parts(value)
    both = dot(table_ref[0], jnp.concatenate([high, low], 1))
    width = value.shape[1]
    return both[:, :width] + both[:, width:] + dot(table_ref[1], high)


def times_table(value, table_ref):
    high, low = parts(value)
    return dot(high, table_ref[0]) + dot(low, table_ref[0]) + dot(high, table_ref[1])


def x_first(pixels_ref, a_ref):
    @pl.loop(0, L // 8)
    def _(g):
        rows = pl.ds(pl.multiple_of(g * 8, 8), 8)
        more = pl.ds(pl.multiple_of(g * 8 + L, 8), 8)
        out = real_dft([pixels_ref[n, rows, :] for n in range(R)])
        a_ref[0, rows, :] = out[0][0]
        a_ref[0, more, :] = out[R // 2][0]
        for u in range(1, UNITS):
            a_ref[u, rows, :] = out[u][0]
            a_ref[u, more, :] = out[u][1]


def x_unit(table_ref, value):
    return table_times(table_ref, value).reshape(16, 2, 8, L)


def x_last(b_ref, out_ref):
    def body(g, top):
        rows = pl.ds(pl.multiple_of(g * 8, 8), 8)
        more = pl.ds(pl.multiple_of(g * 8 + L, 8), 8)
        z = [(b_ref[0, rows, :], None)]
        z += [(b_ref[u, rows, :], b_ref[u, more, :]) for u in range(1, UNITS)]
        z += [(b_ref[0, more, :], None)]
        out = real_dft_back(z)
        for n in range(R):
            out_ref[n, rows, :] = out[n]
        while len(out) > 1:
            out = [jnp.maximum(a, b) for a, b in zip(out[0::2], out[1::2])]
        return jnp.maximum(top, out[0])

    return lax.fori_loop(0, L // 8, body, jnp.full((8, L), -jnp.inf, F32))


def y_forward(tile_ref, twist_ref, lanes_ref, v_ref, own_ref, mirror_ref, special):
    z = complex_dft([(tile_ref[p, 0], tile_ref[p, 1]) for p in range(R)], -1)
    for a in range(R):
        re, im = z[a]
        if a:
            c, s = twist_ref[a, 0], twist_ref[a, 1]
            re, im = re * c + im * s, im * c - re * s
        v_ref[a, :, :L] = re
        v_ref[a, :, L:] = im
    own_ref[...] = times_table(v_ref[...].reshape(R * 8, 2 * L), lanes_ref).reshape(R, 8, 2 * L)

    @pl.when(special)
    def _():
        c, s = twist_ref[R, 0], twist_ref[R, 1]

        @pl.loop(0, R)
        def _(a):
            first = a == 0
            back = lax.rem(R - a, R)
            re, im = v_ref[back, :, :L], -v_ref[back, :, L:]
            mirror_ref[a, :, :L] = jnp.where(first, re, re * c + im * s)
            mirror_ref[a, :, L:] = jnp.where(first, im, im * c - re * s)

        value = mirror_ref[...].reshape(R * 8, 2 * L)
        mirror_ref[...] = times_table(value, lanes_ref).reshape(R, 8, 2 * L)


def phase(pr, pi, our, oi):
    re = pr * our + pi * oi
    im = pi * our - pr * oi
    scale = lax.rsqrt(jnp.maximum(re * re + im * im, FLOOR * FLOOR))
    return re * scale, im * scale


def y_ratio(prior_ref, own_ref, prior_mirror_ref, own_mirror_ref, v_ref, special):
    re, im = phase(prior_ref[:, :, :L], prior_ref[:, :, L:], own_ref[:, :, :L], own_ref[:, :, L:])
    v_ref[:, :, :L] = re
    v_ref[:, :, L:] = im

    @pl.when(special)
    def _():
        def both(ref, mirror, a):
            re, im, mre, mim = ref[a, :, :L], ref[a, :, L:], mirror[a, :, :L], mirror[a, :, L:]
            low = ((re + mre) * 0.5, (im + mim) * 0.5)
            high = ((im - mim) * 0.5, (mre - re) * 0.5)
            return low, high

        packed = lax.broadcasted_iota(jnp.int32, (8, L), 0) == 0

        @pl.loop(0, R)
        def _(a):
            prior_low, prior_high = both(prior_ref, prior_mirror_ref, a)
            own_low, own_high = both(own_ref, own_mirror_ref, a)
            low = phase(*prior_low, *own_low)
            high = phase(*prior_high, *own_high)
            v_ref[a, :, :L] = jnp.where(packed, low[0] - high[1], v_ref[a, :, :L])
            v_ref[a, :, L:] = jnp.where(packed, low[1] + high[0], v_ref[a, :, L:])


def y_back(v_ref, twist_ref, lanes_inv_ref, out_ref):
    v_ref[...] = times_table(v_ref[...].reshape(R * 8, 2 * L), lanes_inv_ref).reshape(R, 8, 2 * L)
    z = []
    for a in range(R):
        re, im = v_ref[a, :, :L], v_ref[a, :, L:]
        if a:
            c, s = twist_ref[a, 0], twist_ref[a, 1]
            re, im = re * c - im * s, im * c + re * s
        z.append((re, im))
    z = complex_dft(z, 1)
    for p in range(R):
        out_ref[p, 0] = z[p][0]
        out_ref[p, 1] = z[p][1]


def here():
    return lax.axis_index("section"), lax.axis_index("row")


def kernel(
    sec_hbm, pre_hbm, fwd_hbm, inv_hbm, lanes_hbm, lanes_inv_hbm, twist_hbm,
    out_ref, peak_ref,
    sec_ref, pre_ref, fwd_ref, inv_ref, lanes_ref, lanes_inv_ref, twist_ref,
    a_ref, b_ref, x_ref, r_ref, y_ref, q_ref, v_ref, spec_ref, mirror_ref, mine_ref, all_ref,
    load_sem, send_sem, there_sem, back_sem, top_sem,
):
    s, p = here()
    me = s * ROW + p
    special = me == 0
    loads = [
        pltpu.make_async_copy(source, target, load_sem.at[i])
        for i, (source, target) in enumerate(
            (
                (sec_hbm, sec_ref),
                (fwd_hbm, fwd_ref),
                (pre_hbm, pre_ref),
                (twist_hbm, twist_ref),
                (lanes_hbm, lanes_ref),
                (lanes_inv_hbm, lanes_inv_ref),
                (inv_hbm, inv_ref),
            )
        )
    ]
    for load in loads:
        load.start()

    bar = pltpu.get_barrier_semaphore()

    def greet(i, _):
        to = ((s + (i >> 5)) & (SEC - 1), (p + i) & (ROW - 1))
        pl.semaphore_signal(bar, inc=1, device_id=to, device_id_type=MESH)
        return 0

    lax.fori_loop(1, DEV, greet, 0, unroll=5)

    def send(group, source_ref, base, target_ref, mark, sem, ready, own):
        if own:
            pltpu.make_async_copy(source_ref.at[base + p], target_ref.at[mark], ready).start()

        def one(i, _):
            to = (p + i) & (ROW - 1)
            pltpu.make_async_remote_copy(
                source_ref.at[base + to], target_ref.at[mark], sem, ready, device_id=(group, to), device_id_type=MESH
            ).start()
            return 0

        lax.fori_loop(1 if own else 0, ROW, one, 0)

    def units(group, from_ref, base):
        for h in range(2):
            u = 2 * group + h
            x_ref[pl.ds(base + h * 16, 16)] = x_unit(fwd_ref.at[u], from_ref[u])

    loads[0].wait()
    x_first(sec_ref, a_ref)
    loads[1].wait()
    units(s, a_ref, s * ROW)
    pl.semaphore_wait(bar, DEV - 1)
    send(s, x_ref, s * ROW, r_ref, me, send_sem.at[0], there_sem.at[0], True)
    loads[2].wait()
    x_first(pre_ref, b_ref)
    units(s, b_ref, DEV)
    send(s, x_ref, DEV, r_ref, DEV + p, send_sem.at[0], there_sem.at[1], True)

    @pl.loop(1, SEC)
    def _(t):
        group = (s + t) & (SEC - 1)
        units(group, a_ref, group * ROW)
        send(group, x_ref, group * ROW, r_ref, me, send_sem.at[0], there_sem.at[t + 1], False)

    for load in loads[3:6]:
        load.wait()

    @pl.loop(0, SEC + 2)
    def _(k):
        @pl.when(k < SEC + 1)
        def _():
            index = jnp.where(k == 1, SEC, (s - jnp.maximum(k - 1, 0)) & (SEC - 1))
            tile = r_ref.at[pl.ds(index * ROW, ROW)]
            pltpu.make_async_copy(tile, tile, there_sem.at[k]).wait()
            y_forward(tile, twist_ref, lanes_ref, v_ref, spec_ref.at[index], mirror_ref.at[index], special)

        @pl.when(k >= 2)
        def _():
            own = (s - k + 2) & (SEC - 1)
            prior = jnp.where(own == 0, SEC, own - 1)
            y_ratio(spec_ref.at[prior], spec_ref.at[own], mirror_ref.at[prior], mirror_ref.at[own], v_ref, special)
            y_back(v_ref, twist_ref, lanes_inv_ref, y_ref.at[pl.ds(own * ROW, ROW)])

            @pl.when(k == 2)
            def _():
                send(s, y_ref, s * ROW, q_ref, me, send_sem.at[1], back_sem.at[0], True)

            @pl.when(k > 2)
            def _():
                send(own, y_ref, own * ROW, q_ref, me, send_sem.at[1], back_sem.at[k - 2], False)

    loads[6].wait()

    @pl.loop(0, SEC)
    def _(m):
        group = (s + m) & (SEC - 1)
        tile = q_ref.at[pl.ds(group * ROW, ROW)]
        pltpu.make_async_copy(tile, tile, back_sem.at[m]).wait()
        for h in range(2):
            u = 2 * group + h
            b_ref[u] = table_times(inv_ref.at[u], q_ref[pl.ds(u * 16, 16)].reshape(2 * L, L))

    top = x_last(b_ref, out_ref)

    mine_ref[...] = top
    all_ref[p] = top

    def tell(i, _):
        to = (p + i) & (ROW - 1)
        pltpu.make_async_remote_copy(
            mine_ref, all_ref.at[p], top_sem.at[0], top_sem.at[1], device_id=(s, to), device_id_type=MESH
        ).start()
        return 0

    lax.fori_loop(1, ROW, tell, 0)

    sent = r_ref.at[pl.ds(0, DEV + ROW - 2)]
    pltpu.make_async_copy(sent, sent, send_sem.at[0]).wait()
    sent = q_ref.at[pl.ds(0, DEV - 1)]
    pltpu.make_async_copy(sent, sent, send_sem.at[1]).wait()
    for i in range(2):
        told = all_ref.at[pl.ds(0, ROW - 1)]
        pltpu.make_async_copy(told, told, top_sem.at[i]).wait()
    peak_ref[...] = jnp.max(all_ref[...], axis=0)


VMEM = pl.BlockSpec(memory_space=pltpu.VMEM)
ANY = pl.BlockSpec(memory_space=pl.ANY)


def f32(*shape):
    return jax.ShapeDtypeStruct(shape, F32)


def local(sections, preceding):
    fwd, inv, lanes, lanes_inv, twist = (jnp.asarray(t) for t in tables())
    args = (sections.reshape(R, L, L), preceding.reshape(R, L, L), fwd, inv, lanes, lanes_inv, twist)
    sem = pltpu.SemaphoreType.DMA
    blocks = lambda count: pltpu.VMEM((count, 2, 8, L), F32)
    surface, peak = pl.pallas_call(
        kernel,
        out_shape=(f32(R, L, L), f32(8, L)),
        in_specs=[ANY] * len(args),
        out_specs=(VMEM, VMEM),
        scratch_shapes=[pltpu.VMEM(v.shape, v.dtype) for v in args]
        + [pltpu.VMEM((UNITS, 2 * L, L), F32)] * 2
        + [blocks(DEV + ROW), blocks(DEV + ROW), blocks(DEV), blocks(DEV)]
        + [pltpu.VMEM((R, 8, 2 * L), F32)]
        + [pltpu.VMEM((SEC + 1, R, 8, 2 * L), F32)] * 2
        + [pltpu.VMEM((8, L), F32), pltpu.VMEM((ROW, 8, L), F32)]
        + [sem((7,)), sem((2,)), sem((SEC + 1,)), sem((SEC,)), sem((2,))],
        compiler_params=pltpu.CompilerParams(vmem_limit_bytes=VMEM_LIMIT, collective_id=1, has_side_effects=True),
    )(*args)
    return surface.reshape(1, N, L), jnp.max(peak).reshape(1)


def solution(mesh):
    in_specs = (P("section", None, "row"), P(None, "row"))
    out_specs = (P("section", None, "row"), P("section"))
    return jax.shard_map(local, mesh=mesh, in_specs=in_specs, out_specs=out_specs, check_vma=False)
```

```python
import functools
import math

import jax
import jax.numpy as jnp
import ml_dtypes
import numpy as np
from jax import lax
from jax.experimental import pallas as pl
from jax.experimental.pallas import tpu as pltpu
from jax.sharding import PartitionSpec as P

MESH = pl.DeviceIdType.MESH
F32 = jnp.float32
BF16 = jnp.bfloat16

N = 4096
R = 32
L = 128
SEC = 8
ROW = 32
DEV = SEC * ROW
PADDED = 512
UNITS = 16
FLOOR = 0.02 * 4096 * 4096
VMEM_LIMIT = 48 << 20


def split(table):
    high = table.astype(ml_dtypes.bfloat16)
    low = (table - high.astype(np.float64)).astype(ml_dtypes.bfloat16)
    return np.stack([high, low], -3)


@functools.lru_cache(None)
def tables():
    n2 = np.arange(L)
    row = np.arange(L)
    fwd = np.zeros((UNITS, 16, 2, 8, 2, L))
    inv = np.zeros((UNITS, 2, L, 16, 2, 8))

    def angles(kx):
        turn = 2 * np.pi / N * (np.outer(kx, n2) % N)
        return np.cos(turn).reshape(-1, 8, L), np.sin(turn).reshape(-1, 8, L)

    for u in range(1, UNITS):
        c, s = angles(u + R * row)
        fwd[u, :, 0, :, 0], fwd[u, :, 0, :, 1] = c, s
        fwd[u, :, 1, :, 0], fwd[u, :, 1, :, 1] = -s, c
        ct, st = np.moveaxis(c, 2, 0), np.moveaxis(s, 2, 0)
        inv[u, 0, :, :, 0], inv[u, 0, :, :, 1] = ct, -st
        inv[u, 1, :, :, 0], inv[u, 1, :, :, 1] = st, ct
    for half, base in ((0, 0), (1, 16)):
        c, s = angles(base + R * np.arange(L // 2))
        js = slice(8 * half, 8 * half + 8)
        ti, tr = -s, c
        bi, br = -2 * s, 2 * c
        if half == 0:
            ti[0, 0] = (-1.0) ** n2
            bi[0, 0] = (-1.0) ** n2
            br[0, 0] = 1.0
        fwd[0, js, 0, :, half], fwd[0, js, 1, :, half] = tr, ti
        inv[0, half, :, js, 0] = np.moveaxis(br, 2, 0)
        inv[0, half, :, js, 1] = np.moveaxis(bi, 2, 0)
    fwd, inv = fwd.reshape(UNITS, 2 * L, 2 * L), inv.reshape(UNITS, 2 * L, 2 * L) / N
    turn = 2 * np.pi / L * (np.outer(row, row) % L)
    c, s = np.cos(turn), np.sin(turn)
    fwd = split(np.concatenate([fwd, np.block([[c, -s], [s, c]])[None]]))
    inv = split(np.concatenate([inv, np.block([[c, s], [-s, c]])[None]]))
    turn = 2 * np.pi / N * np.outer(np.arange(R + 1), row)
    twist = np.stack([np.cos(turn), np.sin(turn)], 1).astype(np.float32)
    twist = np.broadcast_to(twist[:, :, None, :], (R + 1, 2, 8, L)).copy()
    return fwd, inv, np.pad(twist, ((0, PADDED - R - 1), (0, 0), (0, 0), (0, 0)))


def turned(z, k, n, sign):
    k %= n
    re, im = z
    if k == 0:
        return z
    if 4 * k == n:
        return (-im, re) if sign > 0 else (im, -re)
    if 2 * k == n:
        return (-re, -im)
    if 8 * k == n:
        h = math.sqrt(0.5)
        return ((re - im) * h, (re + im) * h) if sign > 0 else ((re + im) * h, (im - re) * h)
    c, s = math.cos(2 * math.pi * k / n), sign * math.sin(2 * math.pi * k / n)
    return (re * c - im * s, re * s + im * c)


def add(a, b):
    return (a[0] + b[0], a[1] + b[1])


def sub(a, b):
    return (a[0] - b[0], a[1] - b[1])


def complex_dft(z, sign):
    n = len(z)
    if n == 1:
        return z
    even, odd = complex_dft(z[0::2], sign), complex_dft(z[1::2], sign)
    out = [None] * n
    for k in range(n // 2):
        t = turned(odd[k], k, n, sign)
        out[k], out[k + n // 2] = add(even[k], t), sub(even[k], t)
    return out


def real_dft(x):
    n = len(x)
    if n == 2:
        return [(x[0] + x[1], None), (x[0] - x[1], None)]
    even, odd = real_dft(x[0::2]), real_dft(x[1::2])
    out = [None] * (n // 2 + 1)
    out[0] = (even[0][0] + odd[0][0], None)
    out[n // 2] = (even[0][0] - odd[0][0], None)
    for k in range(1, n // 4):
        t = turned(odd[k], k, n, -1)
        out[k] = add(even[k], t)
        d = sub(even[k], t)
        out[n // 2 - k] = (d[0], -d[1])
    out[n // 4] = (even[n // 4][0], -odd[n // 4][0])
    return out


def real_dft_back(z):
    n = 2 * (len(z) - 1)
    if n == 2:
        return [z[0][0] + z[1][0], z[0][0] - z[1][0]]
    even, odd = [None] * (n // 4 + 1), [None] * (n // 4 + 1)
    even[0] = (z[0][0] + z[n // 2][0], None)
    odd[0] = (z[0][0] - z[n // 2][0], None)
    for k in range(1, n // 4):
        mirror = (z[n // 2 - k][0], -z[n // 2 - k][1])
        even[k] = add(z[k], mirror)
        odd[k] = turned(sub(z[k], mirror), k, n, 1)
    even[n // 4] = (z[n // 4][0] * 2.0, None)
    odd[n // 4] = (z[n // 4][1] * -2.0, None)
    out = [None] * n
    out[0::2], out[1::2] = real_dft_back(even), real_dft_back(odd)
    return out


def parts(value):
    high = value.astype(BF16)
    return high, (value - high.astype(F32)).astype(BF16)


def dot(a, b):
    return jnp.dot(a, b, preferred_element_type=F32)


def table_times(table_ref, value):
    high, low = parts(value)
    both = dot(table_ref[0], jnp.concatenate([high, low], 1))
    width = value.shape[1]
    return both[:, :width] + both[:, width:] + dot(table_ref[1], high)


def times_table(value, table_ref):
    high, low = parts(value)
    return dot(high, table_ref[0]) + dot(low, table_ref[0]) + dot(high, table_ref[1])


def x_first(pixels_ref, a_ref):
    @pl.loop(0, L // 8)
    def _(g):
        rows = pl.ds(pl.multiple_of(g * 8, 8), 8)
        more = pl.ds(pl.multiple_of(g * 8 + L, 8), 8)
        out = real_dft([pixels_ref[n, rows, :] for n in range(R)])
        a_ref[0, rows, :] = out[0][0]
        a_ref[0, more, :] = out[R // 2][0]
        for u in range(1, UNITS):
            a_ref[u, rows, :] = out[u][0]
            a_ref[u, more, :] = out[u][1]


def x_unit(table_ref, value):
    return table_times(table_ref, value).reshape(16, 2, 8, L)


def x_last(b_ref, out_ref):
    def body(g, top):
        rows = pl.ds(pl.multiple_of(g * 8, 8), 8)
        more = pl.ds(pl.multiple_of(g * 8 + L, 8), 8)
        z = [(b_ref[0, rows, :], None)]
        z += [(b_ref[u, rows, :], b_ref[u, more, :]) for u in range(1, UNITS)]
        z += [(b_ref[0, more, :], None)]
        out = real_dft_back(z)
        for n in range(R):
            out_ref[n, rows, :] = out[n]
        while len(out) > 1:
            out = [jnp.maximum(a, b) for a, b in zip(out[0::2], out[1::2])]
        return jnp.maximum(top, out[0])

    return lax.fori_loop(0, L // 8, body, jnp.full((8, L), -jnp.inf, F32))


def y_forward(tile_ref, twist_ref, lanes_ref, v_ref, own_ref, mirror_ref, special):
    z = complex_dft([(tile_ref[p, 0], tile_ref[p, 1]) for p in range(R)], -1)
    for a in range(R):
        re, im = z[a]
        if a:
            c, s = twist_ref[a, 0], twist_ref[a, 1]
            re, im = re * c + im * s, im * c - re * s
        v_ref[a, :, :L] = re
        v_ref[a, :, L:] = im
    own_ref[...] = times_table(v_ref[...].reshape(R * 8, 2 * L), lanes_ref).reshape(R, 8, 2 * L)

    @pl.when(special)
    def _():
        c, s = twist_ref[R, 0], twist_ref[R, 1]

        @pl.loop(0, R)
        def _(a):
            first = a == 0
            back = lax.rem(R - a, R)
            re, im = v_ref[back, :, :L], -v_ref[back, :, L:]
            mirror_ref[a, :, :L] = jnp.where(first, re, re * c + im * s)
            mirror_ref[a, :, L:] = jnp.where(first, im, im * c - re * s)

        value = mirror_ref[...].reshape(R * 8, 2 * L)
        mirror_ref[...] = times_table(value, lanes_ref).reshape(R, 8, 2 * L)


def phase(pr, pi, our, oi):
    re = pr * our + pi * oi
    im = pi * our - pr * oi
    scale = lax.rsqrt(jnp.maximum(re * re + im * im, FLOOR * FLOOR))
    return re * scale, im * scale


def y_ratio(prior_ref, own_ref, prior_mirror_ref, own_mirror_ref, v_ref, special):
    re, im = phase(prior_ref[:, :, :L], prior_ref[:, :, L:], own_ref[:, :, :L], own_ref[:, :, L:])
    v_ref[:, :, :L] = re
    v_ref[:, :, L:] = im

    @pl.when(special)
    def _():
        def both(ref, mirror, a):
            re, im, mre, mim = ref[a, :, :L], ref[a, :, L:], mirror[a, :, :L], mirror[a, :, L:]
            low = ((re + mre) * 0.5, (im + mim) * 0.5)
            high = ((im - mim) * 0.5, (mre - re) * 0.5)
            return low, high

        packed = lax.broadcasted_iota(jnp.int32, (8, L), 0) == 0

        @pl.loop(0, R)
        def _(a):
            prior_low, prior_high = both(prior_ref, prior_mirror_ref, a)
            own_low, own_high = both(own_ref, own_mirror_ref, a)
            low = phase(*prior_low, *own_low)
            high = phase(*prior_high, *own_high)
            v_ref[a, :, :L] = jnp.where(packed, low[0] - high[1], v_ref[a, :, :L])
            v_ref[a, :, L:] = jnp.where(packed, low[1] + high[0], v_ref[a, :, L:])


def y_back(v_ref, twist_ref, lanes_inv_ref, out_ref):
    v_ref[...] = times_table(v_ref[...].reshape(R * 8, 2 * L), lanes_inv_ref).reshape(R, 8, 2 * L)
    z = []
    for a in range(R):
        re, im = v_ref[a, :, :L], v_ref[a, :, L:]
        if a:
            c, s = twist_ref[a, 0], twist_ref[a, 1]
            re, im = re * c - im * s, im * c + re * s
        z.append((re, im))
    z = complex_dft(z, 1)
    for p in range(R):
        out_ref[p, 0] = z[p][0]
        out_ref[p, 1] = z[p][1]


def here():
    return lax.axis_index("section"), lax.axis_index("row")


def partner(p, j):
    zj, yj, cj = j >> 3, (j >> 1) & 3, j & 1
    dz, dy = zj ^ (zj >> 1) ^ 2, yj ^ (yj >> 1) ^ 2
    z, y, core = ((p >> 3) + dz) & 3, ((p >> 1) + dy) & 3, (p & 1) ^ (1 - cj)
    return z * 8 + y * 2 + core


def kernel(
    sec_hbm, pre_hbm, fwd_hbm, inv_hbm, twist_hbm,
    out_ref, peak_ref,
    sec_ref, pre_ref, fwd_ref, inv_ref, twist_ref,
    a_ref, b_ref, x_ref, r_ref, y_ref, q_ref, v_ref, spec_ref, mirror_ref, mine_ref, all_ref,
    load_sem, send_sem, there_sem, back_sem, top_sem, go_sem,
):
    s, p = here()
    me = s * ROW + p
    special = me == 0
    loads = [
        pltpu.make_async_copy(source, target, load_sem.at[i])
        for i, (source, target) in enumerate(
            (
                (sec_hbm, sec_ref),
                (fwd_hbm, fwd_ref),
                (pre_hbm, pre_ref),
                (twist_hbm.at[pl.ds(0, R + 1)], twist_ref),
                (inv_hbm, inv_ref),
            )
        )
    ]
    loads[0].start()
    loads[1].start()

    bar = pltpu.get_barrier_semaphore()

    def greet(j, _):
        pl.semaphore_signal(bar, inc=1, device_id=(s, partner(p, j)), device_id_type=MESH)
        return 0

    lax.fori_loop(0, ROW - 1, greet, 0)

    def send(group, source_ref, base, target_ref, mark, sem, ready, own):
        if own:
            pltpu.make_async_copy(source_ref.at[base + p], target_ref.at[mark], ready).start()

        def one(j, _):
            to = partner(p, j)
            pltpu.make_async_remote_copy(
                source_ref.at[base + to], target_ref.at[mark], sem, ready, device_id=(group, to), device_id_type=MESH
            ).start()
            return 0

        lax.fori_loop(0, ROW - 1 if own else ROW, one, 0)

    def units(group, from_ref, base):
        for h in range(2):
            u = 2 * group + h
            x_ref[pl.ds(base + h * 16, 16)] = x_unit(fwd_ref.at[u], from_ref[u])

    loads[0].wait()
    for load in loads[2:]:
        load.start()
    x_first(sec_ref, a_ref)
    loads[1].wait()
    units(s, a_ref, s * ROW)

    @pl.when(p != 1)
    def _():
        pl.semaphore_wait(bar, ROW - 1)

    @pl.when(p == 0)
    def _():
        for t in range(1, SEC):
            pl.semaphore_signal(bar, inc=1, device_id=((s + t) & (SEC - 1), 1), device_id_type=MESH)

    @pl.when(p == 1)
    def _():
        pl.semaphore_wait(bar, ROW - 1 + SEC - 1)

        def release(j, _):
            pl.semaphore_signal(go_sem, inc=1, device_id=(s, partner(p, j)), device_id_type=MESH)
            return 0

        lax.fori_loop(0, ROW - 1, release, 0)

    send(s, x_ref, s * ROW, r_ref, me, send_sem.at[0], there_sem.at[0], True)
    loads[2].wait()
    x_first(pre_ref, b_ref)
    units(s, b_ref, DEV)
    send(s, x_ref, DEV, r_ref, DEV + p, send_sem.at[0], there_sem.at[1], True)

    @pl.when(p != 1)
    def _():
        pl.semaphore_wait(go_sem, 1)

    @pl.loop(1, SEC)
    def _(t):
        group = (s + t) & (SEC - 1)
        units(group, a_ref, group * ROW)
        send(group, x_ref, group * ROW, r_ref, me, send_sem.at[0], there_sem.at[t + 1], False)

    for load in loads[3:]:
        load.wait()
    lanes_ref, lanes_inv_ref = fwd_ref.at[UNITS], inv_ref.at[UNITS]

    @pl.loop(0, SEC + 2)
    def _(k):
        @pl.when(k < SEC + 1)
        def _():
            index = jnp.where(k == 1, SEC, (s - jnp.maximum(k - 1, 0)) & (SEC - 1))
            tile = r_ref.at[pl.ds(index * ROW, ROW)]
            pltpu.make_async_copy(tile, tile, there_sem.at[k]).wait()
            y_forward(tile, twist_ref, lanes_ref, v_ref, spec_ref.at[index], mirror_ref.at[index], special)

        @pl.when(k >= 2)
        def _():
            own = (s - k + 2) & (SEC - 1)
            prior = jnp.where(own == 0, SEC, own - 1)
            y_ratio(spec_ref.at[prior], spec_ref.at[own], mirror_ref.at[prior], mirror_ref.at[own], v_ref, special)
            y_back(v_ref, twist_ref, lanes_inv_ref, y_ref.at[pl.ds(own * ROW, ROW)])

            @pl.when(k == 2)
            def _():
                send(s, y_ref, s * ROW, q_ref, me, send_sem.at[1], back_sem.at[0], True)

            @pl.when(k > 2)
            def _():
                send(own, y_ref, own * ROW, q_ref, me, send_sem.at[1], back_sem.at[k - 2], False)

    @pl.loop(0, SEC)
    def _(m):
        group = (s + m) & (SEC - 1)
        tile = q_ref.at[pl.ds(group * ROW, ROW)]
        pltpu.make_async_copy(tile, tile, back_sem.at[m]).wait()
        for h in range(2):
            u = 2 * group + h
            b_ref[u] = table_times(inv_ref.at[u], q_ref[pl.ds(u * 16, 16)].reshape(2 * L, L))

    top = x_last(b_ref, out_ref)

    mine_ref[...] = top
    all_ref[p] = top

    def tell(j, _):
        to = partner(p, j)
        pltpu.make_async_remote_copy(
            mine_ref, all_ref.at[p], top_sem.at[0], top_sem.at[1], device_id=(s, to), device_id_type=MESH
        ).start()
        return 0

    lax.fori_loop(0, ROW - 1, tell, 0)

    sent = r_ref.at[pl.ds(0, DEV + ROW - 2)]
    pltpu.make_async_copy(sent, sent, send_sem.at[0]).wait()
    sent = q_ref.at[pl.ds(0, DEV - 1)]
    pltpu.make_async_copy(sent, sent, send_sem.at[1]).wait()
    for i in range(2):
        told = all_ref.at[pl.ds(0, ROW - 1)]
        pltpu.make_async_copy(told, told, top_sem.at[i]).wait()
    peak_ref[0] = jnp.max(all_ref[...])


VMEM = pl.BlockSpec(memory_space=pltpu.VMEM)
SMEM = pl.BlockSpec(memory_space=pltpu.SMEM)
HBM = pl.BlockSpec(memory_space=pltpu.HBM)


def f32(*shape):
    return jax.ShapeDtypeStruct(shape, F32)


def local(sections, preceding):
    fwd, inv, twist = (jnp.asarray(t) for t in tables())
    args = (sections.reshape(R, L, L), preceding.reshape(R, L, L), fwd, inv, twist)
    sem = pltpu.SemaphoreType.DMA
    blocks = lambda count: pltpu.VMEM((count, 2, 8, L), F32)
    surface, peak = pl.pallas_call(
        kernel,
        out_shape=(f32(R, L, L), f32(1)),
        in_specs=[HBM] * len(args),
        out_specs=(VMEM, SMEM),
        scratch_shapes=[pltpu.VMEM(v.shape, v.dtype) for v in args[:4]]
        + [pltpu.VMEM((R + 1, 2, 8, L), F32)]
        + [pltpu.VMEM((UNITS, 2 * L, L), F32)] * 2
        + [blocks(DEV + ROW), blocks(DEV + ROW), blocks(DEV), blocks(DEV)]
        + [pltpu.VMEM((R, 8, 2 * L), F32)]
        + [pltpu.VMEM((SEC + 1, R, 8, 2 * L), F32)] * 2
        + [pltpu.VMEM((8, L), F32), pltpu.VMEM((ROW, 8, L), F32)]
        + [sem((5,)), sem((2,)), sem((SEC + 1,)), sem((SEC,)), sem((2,)), pltpu.SemaphoreType.REGULAR],
        compiler_params=pltpu.CompilerParams(vmem_limit_bytes=VMEM_LIMIT, collective_id=1, has_side_effects=True),
    )(*args)
    return surface.reshape(1, N, L), peak


def solution(mesh):
    in_specs = (P("section", None, "row"), P(None, "row"))
    out_specs = (P("section", None, "row"), P("section"))
    return jax.shard_map(local, mesh=mesh, in_specs=in_specs, out_specs=out_specs, check_vma=False)
```

```python
import functools
import math

import jax
import jax.numpy as jnp
import ml_dtypes
import numpy as np
from jax import lax
from jax.experimental import pallas as pl
from jax.experimental.pallas import tpu as pltpu
from jax.sharding import PartitionSpec as P

MESH = pl.DeviceIdType.MESH
F32 = jnp.float32
BF16 = jnp.bfloat16

N = 4096
R = 32
L = 128
SEC = 8
ROW = 32
DEV = SEC * ROW
PADDED = 512
UNITS = 16
FLOOR = 0.02 * 4096 * 4096
VMEM_LIMIT = 50 << 20


def split(table):
    high = table.astype(ml_dtypes.bfloat16)
    low = (table - high.astype(np.float64)).astype(ml_dtypes.bfloat16)
    return np.stack([high, low], -3)


@functools.lru_cache(None)
def tables():
    n2 = np.arange(L)
    row = np.arange(L)
    fwd = np.zeros((UNITS, 16, 2, 8, 2, L))
    inv = np.zeros((UNITS, 2, L, 16, 2, 8))

    def angles(kx):
        turn = 2 * np.pi / N * (np.outer(kx, n2) % N)
        return np.cos(turn).reshape(-1, 8, L), np.sin(turn).reshape(-1, 8, L)

    for u in range(1, UNITS):
        c, s = angles(u + R * row)
        fwd[u, :, 0, :, 0], fwd[u, :, 0, :, 1] = c, s
        fwd[u, :, 1, :, 0], fwd[u, :, 1, :, 1] = -s, c
        ct, st = np.moveaxis(c, 2, 0), np.moveaxis(s, 2, 0)
        inv[u, 0, :, :, 0], inv[u, 0, :, :, 1] = ct, -st
        inv[u, 1, :, :, 0], inv[u, 1, :, :, 1] = st, ct
    for half, base in ((0, 0), (1, 16)):
        c, s = angles(base + R * np.arange(L // 2))
        js = slice(8 * half, 8 * half + 8)
        ti, tr = -s, c
        bi, br = -2 * s, 2 * c
        if half == 0:
            ti[0, 0] = (-1.0) ** n2
            bi[0, 0] = (-1.0) ** n2
            br[0, 0] = 1.0
        fwd[0, js, 0, :, half], fwd[0, js, 1, :, half] = tr, ti
        inv[0, half, :, js, 0] = np.moveaxis(br, 2, 0)
        inv[0, half, :, js, 1] = np.moveaxis(bi, 2, 0)
    fwd, inv = fwd.reshape(UNITS, 2 * L, 2 * L), inv.reshape(UNITS, 2 * L, 2 * L) / N
    turn = 2 * np.pi / L * (np.outer(row, row) % L)
    c, s = np.cos(turn), np.sin(turn)
    fwd = split(np.concatenate([fwd, np.block([[c, -s], [s, c]])[None]]))
    inv = split(np.concatenate([inv, np.block([[c, s], [-s, c]])[None]]))
    turn = 2 * np.pi / N * np.outer(np.arange(R + 1), row)
    twist = np.stack([np.cos(turn), np.sin(turn)], 1).astype(np.float32)
    twist = np.broadcast_to(twist[:, :, None, :], (R + 1, 2, 8, L)).copy()
    return fwd, inv, np.pad(twist, ((0, PADDED - R - 1), (0, 0), (0, 0), (0, 0)))


def turned(z, k, n, sign):
    k %= n
    re, im = z
    if k == 0:
        return z
    if 4 * k == n:
        return (-im, re) if sign > 0 else (im, -re)
    if 2 * k == n:
        return (-re, -im)
    if 8 * k == n:
        h = math.sqrt(0.5)
        return ((re - im) * h, (re + im) * h) if sign > 0 else ((re + im) * h, (im - re) * h)
    c, s = math.cos(2 * math.pi * k / n), sign * math.sin(2 * math.pi * k / n)
    return (re * c - im * s, re * s + im * c)


def add(a, b):
    return (a[0] + b[0], a[1] + b[1])


def sub(a, b):
    return (a[0] - b[0], a[1] - b[1])


def complex_dft(z, sign):
    n = len(z)
    if n == 1:
        return z
    even, odd = complex_dft(z[0::2], sign), complex_dft(z[1::2], sign)
    out = [None] * n
    for k in range(n // 2):
        t = turned(odd[k], k, n, sign)
        out[k], out[k + n // 2] = add(even[k], t), sub(even[k], t)
    return out


def real_dft(x):
    n = len(x)
    if n == 2:
        return [(x[0] + x[1], None), (x[0] - x[1], None)]
    even, odd = real_dft(x[0::2]), real_dft(x[1::2])
    out = [None] * (n // 2 + 1)
    out[0] = (even[0][0] + odd[0][0], None)
    out[n // 2] = (even[0][0] - odd[0][0], None)
    for k in range(1, n // 4):
        t = turned(odd[k], k, n, -1)
        out[k] = add(even[k], t)
        d = sub(even[k], t)
        out[n // 2 - k] = (d[0], -d[1])
    out[n // 4] = (even[n // 4][0], -odd[n // 4][0])
    return out


def real_dft_back(z):
    n = 2 * (len(z) - 1)
    if n == 2:
        return [z[0][0] + z[1][0], z[0][0] - z[1][0]]
    even, odd = [None] * (n // 4 + 1), [None] * (n // 4 + 1)
    even[0] = (z[0][0] + z[n // 2][0], None)
    odd[0] = (z[0][0] - z[n // 2][0], None)
    for k in range(1, n // 4):
        mirror = (z[n // 2 - k][0], -z[n // 2 - k][1])
        even[k] = add(z[k], mirror)
        odd[k] = turned(sub(z[k], mirror), k, n, 1)
    even[n // 4] = (z[n // 4][0] * 2.0, None)
    odd[n // 4] = (z[n // 4][1] * -2.0, None)
    out = [None] * n
    out[0::2], out[1::2] = real_dft_back(even), real_dft_back(odd)
    return out


def parts(value):
    high = value.astype(BF16)
    return high, (value - high.astype(F32)).astype(BF16)


def dot(a, b):
    return jnp.dot(a, b, preferred_element_type=F32)


def table_times(table_ref, value):
    high, low = parts(value)
    both = dot(table_ref[0], jnp.concatenate([high, low], 1))
    width = value.shape[1]
    return both[:, :width] + both[:, width:] + dot(table_ref[1], high)


def times_table(value, table_ref):
    high, low = parts(value)
    return dot(high, table_ref[0]) + dot(low, table_ref[0]) + dot(high, table_ref[1])


def x_first(pixels_ref, a_ref):
    @pl.loop(0, L // 8)
    def _(g):
        rows = pl.ds(pl.multiple_of(g * 8, 8), 8)
        more = pl.ds(pl.multiple_of(g * 8 + L, 8), 8)
        out = real_dft([pixels_ref[n, rows, :] for n in range(R)])
        a_ref[0, rows, :] = out[0][0]
        a_ref[0, more, :] = out[R // 2][0]
        for u in range(1, UNITS):
            a_ref[u, rows, :] = out[u][0]
            a_ref[u, more, :] = out[u][1]


def x_unit(table_ref, value):
    return table_times(table_ref, value).reshape(16, 2, 8, L)


def x_last(b_ref, out_ref):
    def body(g, top):
        rows = pl.ds(pl.multiple_of(g * 8, 8), 8)
        more = pl.ds(pl.multiple_of(g * 8 + L, 8), 8)
        z = [(b_ref[0, rows, :], None)]
        z += [(b_ref[u, rows, :], b_ref[u, more, :]) for u in range(1, UNITS)]
        z += [(b_ref[0, more, :], None)]
        out = real_dft_back(z)
        for n in range(R):
            out_ref[n, rows, :] = out[n]
        while len(out) > 1:
            out = [jnp.maximum(a, b) for a, b in zip(out[0::2], out[1::2])]
        return jnp.maximum(top, out[0])

    return lax.fori_loop(0, L // 8, body, jnp.full((8, L), -jnp.inf, F32))


def y_forward(tile_ref, twist_ref, lanes_ref, v_ref, own_ref, mirror_ref, special):
    z = complex_dft([(tile_ref[p, 0], tile_ref[p, 1]) for p in range(R)], -1)
    for a in range(R):
        re, im = z[a]
        if a:
            c, s = twist_ref[a, 0], twist_ref[a, 1]
            re, im = re * c + im * s, im * c - re * s
        v_ref[a, :, :L] = re
        v_ref[a, :, L:] = im
    own_ref[...] = times_table(v_ref[...].reshape(R * 8, 2 * L), lanes_ref).reshape(R, 8, 2 * L)

    @pl.when(special)
    def _():
        c, s = twist_ref[R, 0], twist_ref[R, 1]

        @pl.loop(0, R)
        def _(a):
            first = a == 0
            back = lax.rem(R - a, R)
            re, im = v_ref[back, :, :L], -v_ref[back, :, L:]
            mirror_ref[a, :, :L] = jnp.where(first, re, re * c + im * s)
            mirror_ref[a, :, L:] = jnp.where(first, im, im * c - re * s)

        value = mirror_ref[...].reshape(R * 8, 2 * L)
        mirror_ref[...] = times_table(value, lanes_ref).reshape(R, 8, 2 * L)


def phase(pr, pi, our, oi):
    re = pr * our + pi * oi
    im = pi * our - pr * oi
    scale = lax.rsqrt(jnp.maximum(re * re + im * im, FLOOR * FLOOR))
    return re * scale, im * scale


def y_ratio(prior_ref, own_ref, prior_mirror_ref, own_mirror_ref, v_ref, special):
    re, im = phase(prior_ref[:, :, :L], prior_ref[:, :, L:], own_ref[:, :, :L], own_ref[:, :, L:])
    v_ref[:, :, :L] = re
    v_ref[:, :, L:] = im

    @pl.when(special)
    def _():
        def both(ref, mirror, a):
            re, im, mre, mim = ref[a, :, :L], ref[a, :, L:], mirror[a, :, :L], mirror[a, :, L:]
            low = ((re + mre) * 0.5, (im + mim) * 0.5)
            high = ((im - mim) * 0.5, (mre - re) * 0.5)
            return low, high

        packed = lax.broadcasted_iota(jnp.int32, (8, L), 0) == 0

        @pl.loop(0, R)
        def _(a):
            prior_low, prior_high = both(prior_ref, prior_mirror_ref, a)
            own_low, own_high = both(own_ref, own_mirror_ref, a)
            low = phase(*prior_low, *own_low)
            high = phase(*prior_high, *own_high)
            v_ref[a, :, :L] = jnp.where(packed, low[0] - high[1], v_ref[a, :, :L])
            v_ref[a, :, L:] = jnp.where(packed, low[1] + high[0], v_ref[a, :, L:])


def y_back(v_ref, twist_ref, lanes_inv_ref, out_ref):
    v_ref[...] = times_table(v_ref[...].reshape(R * 8, 2 * L), lanes_inv_ref).reshape(R, 8, 2 * L)
    z = []
    for a in range(R):
        re, im = v_ref[a, :, :L], v_ref[a, :, L:]
        if a:
            c, s = twist_ref[a, 0], twist_ref[a, 1]
            re, im = re * c - im * s, im * c + re * s
        z.append((re, im))
    z = complex_dft(z, 1)
    for p in range(R):
        out_ref[p, 0] = z[p][0]
        out_ref[p, 1] = z[p][1]


def here():
    return lax.axis_index("section"), lax.axis_index("row")


def partner(p, j):
    zj, yj, cj = j >> 3, (j >> 1) & 3, j & 1
    dz, dy = zj ^ (zj >> 1) ^ 2, yj ^ (yj >> 1) ^ 2
    z, y, core = ((p >> 3) + dz) & 3, ((p >> 1) + dy) & 3, (p & 1) ^ (1 - cj)
    return z * 8 + y * 2 + core


def kernel(
    sec_hbm, pre_hbm, fwd_hbm, inv_hbm, twist_hbm,
    out_ref, peak_ref,
    sec_ref, pre_ref, fwd_ref, inv_ref, twist_ref,
    near_ref, a_ref, b_ref, x_ref, r_ref, y_ref, q_ref, v_ref, spec_ref, mirror_ref, mine_ref, all_ref,
    load_sem, send_sem, there_sem, back_sem, top_sem, go_sem,
):
    s, p = here()
    me = s * ROW + p
    special = me == 0
    loads = [
        pltpu.make_async_copy(source, target, load_sem.at[i])
        for i, (source, target) in enumerate(
            (
                (sec_hbm, sec_ref),
                (fwd_hbm.at[pl.ds(2 * s, 2)], near_ref),
                (pre_hbm, pre_ref),
                (fwd_hbm, fwd_ref),
                (twist_hbm.at[pl.ds(0, R + 1)], twist_ref),
                (inv_hbm, inv_ref),
            )
        )
    ]
    loads[0].start()
    loads[1].start()

    bar = pltpu.get_barrier_semaphore()

    def greet(j, _):
        pl.semaphore_signal(bar, inc=1, device_id=(s, partner(p, j)), device_id_type=MESH)
        return 0

    lax.fori_loop(0, ROW - 1, greet, 0)

    def send(group, source_ref, base, target_ref, mark, sem, ready, own):
        if own:
            pltpu.make_async_copy(source_ref.at[base + p], target_ref.at[mark], ready).start()

        def one(j, _):
            to = partner(p, j)
            pltpu.make_async_remote_copy(
                source_ref.at[base + to], target_ref.at[mark], sem, ready, device_id=(group, to), device_id_type=MESH
            ).start()
            return 0

        lax.fori_loop(0, ROW - 1 if own else ROW, one, 0)

    def units(group, from_ref, base, table_ref=None):
        for h in range(2):
            u = 2 * group + h
            table = fwd_ref.at[u] if table_ref is None else table_ref.at[h]
            x_ref[pl.ds(base + h * 16, 16)] = x_unit(table, from_ref[u])

    loads[0].wait()
    for load in loads[2:]:
        load.start()
    x_first(sec_ref, a_ref)
    loads[1].wait()
    units(s, a_ref, s * ROW, near_ref)

    second = (p & 1) == 1

    @pl.when(jnp.logical_not(second))
    def _():
        pl.semaphore_wait(bar, ROW - 1)
        for t in range(1, SEC):
            pl.semaphore_signal(bar, inc=1, device_id=((s + t) & (SEC - 1), p + 1), device_id_type=MESH)

    @pl.when(second)
    def _():
        pl.semaphore_wait(bar, ROW - 1 + SEC - 1)
        pl.semaphore_signal(go_sem, inc=1, device_id=(s, p - 1), device_id_type=MESH)

    send(s, x_ref, s * ROW, r_ref, me, send_sem.at[0], there_sem.at[0], True)
    loads[2].wait()
    x_first(pre_ref, b_ref)
    units(s, b_ref, DEV, near_ref)
    send(s, x_ref, DEV, r_ref, DEV + p, send_sem.at[0], there_sem.at[1], True)

    @pl.when(jnp.logical_not(second))
    def _():
        pl.semaphore_wait(go_sem, 1)

    loads[3].wait()

    @pl.loop(1, SEC)
    def _(t):
        group = (s + t) & (SEC - 1)
        units(group, a_ref, group * ROW)
        send(group, x_ref, group * ROW, r_ref, me, send_sem.at[0], there_sem.at[t + 1], False)

    for load in loads[4:]:
        load.wait()
    lanes_ref, lanes_inv_ref = fwd_ref.at[UNITS], inv_ref.at[UNITS]

    @pl.loop(0, SEC + 2)
    def _(k):
        @pl.when(k < SEC + 1)
        def _():
            index = jnp.where(k == 1, SEC, (s - jnp.maximum(k - 1, 0)) & (SEC - 1))
            tile = r_ref.at[pl.ds(index * ROW, ROW)]
            pltpu.make_async_copy(tile, tile, there_sem.at[k]).wait()
            y_forward(tile, twist_ref, lanes_ref, v_ref, spec_ref.at[index], mirror_ref.at[index], special)

        @pl.when(k >= 2)
        def _():
            own = (s - k + 2) & (SEC - 1)
            prior = jnp.where(own == 0, SEC, own - 1)
            y_ratio(spec_ref.at[prior], spec_ref.at[own], mirror_ref.at[prior], mirror_ref.at[own], v_ref, special)
            y_back(v_ref, twist_ref, lanes_inv_ref, y_ref.at[pl.ds(own * ROW, ROW)])

            @pl.when(k == 2)
            def _():
                send(s, y_ref, s * ROW, q_ref, me, send_sem.at[1], back_sem.at[0], True)

            @pl.when(k > 2)
            def _():
                send(own, y_ref, own * ROW, q_ref, me, send_sem.at[1], back_sem.at[k - 2], False)

    @pl.loop(0, SEC)
    def _(m):
        group = (s + m) & (SEC - 1)
        tile = q_ref.at[pl.ds(group * ROW, ROW)]
        pltpu.make_async_copy(tile, tile, back_sem.at[m]).wait()
        for h in range(2):
            u = 2 * group + h
            b_ref[u] = table_times(inv_ref.at[u], q_ref[pl.ds(u * 16, 16)].reshape(2 * L, L))

    top = x_last(b_ref, out_ref)

    mine_ref[...] = top
    all_ref[p] = top

    def tell(j, _):
        to = partner(p, j)
        pltpu.make_async_remote_copy(
            mine_ref, all_ref.at[p], top_sem.at[0], top_sem.at[1], device_id=(s, to), device_id_type=MESH
        ).start()
        return 0

    lax.fori_loop(0, ROW - 1, tell, 0)

    sent = r_ref.at[pl.ds(0, DEV + ROW - 2)]
    pltpu.make_async_copy(sent, sent, send_sem.at[0]).wait()
    sent = q_ref.at[pl.ds(0, DEV - 1)]
    pltpu.make_async_copy(sent, sent, send_sem.at[1]).wait()
    for i in range(2):
        told = all_ref.at[pl.ds(0, ROW - 1)]
        pltpu.make_async_copy(told, told, top_sem.at[i]).wait()
    peak_ref[0] = jnp.max(all_ref[...])


VMEM = pl.BlockSpec(memory_space=pltpu.VMEM)
SMEM = pl.BlockSpec(memory_space=pltpu.SMEM)
HBM = pl.BlockSpec(memory_space=pltpu.HBM)


def f32(*shape):
    return jax.ShapeDtypeStruct(shape, F32)


def local(sections, preceding):
    fwd, inv, twist = (jnp.asarray(t) for t in tables())
    args = (sections.reshape(R, L, L), preceding.reshape(R, L, L), fwd, inv, twist)
    sem = pltpu.SemaphoreType.DMA
    blocks = lambda count: pltpu.VMEM((count, 2, 8, L), F32)
    surface, peak = pl.pallas_call(
        kernel,
        out_shape=(f32(R, L, L), f32(1)),
        in_specs=[HBM] * len(args),
        out_specs=(VMEM, SMEM),
        scratch_shapes=[pltpu.VMEM(v.shape, v.dtype) for v in args[:4]]
        + [pltpu.VMEM((R + 1, 2, 8, L), F32), pltpu.VMEM((2, 2, 2 * L, 2 * L), BF16)]
        + [pltpu.VMEM((UNITS, 2 * L, L), F32)] * 2
        + [blocks(DEV + ROW), blocks(DEV + ROW), blocks(DEV), blocks(DEV)]
        + [pltpu.VMEM((R, 8, 2 * L), F32)]
        + [pltpu.VMEM((SEC + 1, R, 8, 2 * L), F32)] * 2
        + [pltpu.VMEM((8, L), F32), pltpu.VMEM((ROW, 8, L), F32)]
        + [sem((6,)), sem((2,)), sem((SEC + 1,)), sem((SEC,)), sem((2,)), pltpu.SemaphoreType.REGULAR],
        compiler_params=pltpu.CompilerParams(vmem_limit_bytes=VMEM_LIMIT, collective_id=1, has_side_effects=True),
    )(*args)
    return surface.reshape(1, N, L), peak


def solution(mesh):
    in_specs = (P("section", None, "row"), P(None, "row"))
    out_specs = (P("section", None, "row"), P("section"))
    return jax.shard_map(local, mesh=mesh, in_specs=in_specs, out_specs=out_specs, check_vma=False)
```

```python
import functools
import math

import jax
import jax.numpy as jnp
import ml_dtypes
import numpy as np
from jax import lax
from jax.experimental import pallas as pl
from jax.experimental.pallas import tpu as pltpu
from jax.sharding import PartitionSpec as P

MESH = pl.DeviceIdType.MESH
F32 = jnp.float32
BF16 = jnp.bfloat16

N = 4096
R = 32
L = 128
SEC = 8
ROW = 32
DEV = SEC * ROW
PADDED = 512
AHEAD = 3
UNITS = 16
FLOOR = 0.02 * 4096 * 4096
VMEM_LIMIT = 50 << 20


def split(table):
    high = table.astype(ml_dtypes.bfloat16)
    low = (table - high.astype(np.float64)).astype(ml_dtypes.bfloat16)
    return np.stack([high, low], -3)


@functools.lru_cache(None)
def tables():
    n2 = np.arange(L)
    row = np.arange(L)
    fwd = np.zeros((UNITS, 16, 2, 8, 2, L))
    inv = np.zeros((UNITS, 2, L, 16, 2, 8))

    def angles(kx):
        turn = 2 * np.pi / N * (np.outer(kx, n2) % N)
        return np.cos(turn).reshape(-1, 8, L), np.sin(turn).reshape(-1, 8, L)

    for u in range(1, UNITS):
        c, s = angles(u + R * row)
        fwd[u, :, 0, :, 0], fwd[u, :, 0, :, 1] = c, s
        fwd[u, :, 1, :, 0], fwd[u, :, 1, :, 1] = -s, c
        ct, st = np.moveaxis(c, 2, 0), np.moveaxis(s, 2, 0)
        inv[u, 0, :, :, 0], inv[u, 0, :, :, 1] = ct, -st
        inv[u, 1, :, :, 0], inv[u, 1, :, :, 1] = st, ct
    for half, base in ((0, 0), (1, 16)):
        c, s = angles(base + R * np.arange(L // 2))
        js = slice(8 * half, 8 * half + 8)
        ti, tr = -s, c
        bi, br = -2 * s, 2 * c
        if half == 0:
            ti[0, 0] = (-1.0) ** n2
            bi[0, 0] = (-1.0) ** n2
            br[0, 0] = 1.0
        fwd[0, js, 0, :, half], fwd[0, js, 1, :, half] = tr, ti
        inv[0, half, :, js, 0] = np.moveaxis(br, 2, 0)
        inv[0, half, :, js, 1] = np.moveaxis(bi, 2, 0)
    fwd, inv = fwd.reshape(UNITS, 2 * L, 2 * L), inv.reshape(UNITS, 2 * L, 2 * L) / N
    turn = 2 * np.pi / L * (np.outer(row, row) % L)
    c, s = np.cos(turn), np.sin(turn)
    fwd = split(np.concatenate([fwd, np.block([[c, -s], [s, c]])[None]]))
    inv = split(np.concatenate([inv, np.block([[c, s], [-s, c]])[None]]))
    turn = 2 * np.pi / N * np.outer(np.arange(R + 1), row)
    twist = np.stack([np.cos(turn), np.sin(turn)], 1).astype(np.float32)
    twist = np.broadcast_to(twist[:, :, None, :], (R + 1, 2, 8, L)).copy()
    return fwd, inv, np.pad(twist, ((0, PADDED - R - 1), (0, 0), (0, 0), (0, 0)))


def turned(z, k, n, sign):
    k %= n
    re, im = z
    if k == 0:
        return z
    if 4 * k == n:
        return (-im, re) if sign > 0 else (im, -re)
    if 2 * k == n:
        return (-re, -im)
    if 8 * k == n:
        h = math.sqrt(0.5)
        return ((re - im) * h, (re + im) * h) if sign > 0 else ((re + im) * h, (im - re) * h)
    c, s = math.cos(2 * math.pi * k / n), sign * math.sin(2 * math.pi * k / n)
    return (re * c - im * s, re * s + im * c)


def add(a, b):
    return (a[0] + b[0], a[1] + b[1])


def sub(a, b):
    return (a[0] - b[0], a[1] - b[1])


def complex_dft(z, sign):
    n = len(z)
    if n == 1:
        return z
    even, odd = complex_dft(z[0::2], sign), complex_dft(z[1::2], sign)
    out = [None] * n
    for k in range(n // 2):
        t = turned(odd[k], k, n, sign)
        out[k], out[k + n // 2] = add(even[k], t), sub(even[k], t)
    return out


def real_dft(x):
    n = len(x)
    if n == 2:
        return [(x[0] + x[1], None), (x[0] - x[1], None)]
    even, odd = real_dft(x[0::2]), real_dft(x[1::2])
    out = [None] * (n // 2 + 1)
    out[0] = (even[0][0] + odd[0][0], None)
    out[n // 2] = (even[0][0] - odd[0][0], None)
    for k in range(1, n // 4):
        t = turned(odd[k], k, n, -1)
        out[k] = add(even[k], t)
        d = sub(even[k], t)
        out[n // 2 - k] = (d[0], -d[1])
    out[n // 4] = (even[n // 4][0], -odd[n // 4][0])
    return out


def real_dft_back(z):
    n = 2 * (len(z) - 1)
    if n == 2:
        return [z[0][0] + z[1][0], z[0][0] - z[1][0]]
    even, odd = [None] * (n // 4 + 1), [None] * (n // 4 + 1)
    even[0] = (z[0][0] + z[n // 2][0], None)
    odd[0] = (z[0][0] - z[n // 2][0], None)
    for k in range(1, n // 4):
        mirror = (z[n // 2 - k][0], -z[n // 2 - k][1])
        even[k] = add(z[k], mirror)
        odd[k] = turned(sub(z[k], mirror), k, n, 1)
    even[n // 4] = (z[n // 4][0] * 2.0, None)
    odd[n // 4] = (z[n // 4][1] * -2.0, None)
    out = [None] * n
    out[0::2], out[1::2] = real_dft_back(even), real_dft_back(odd)
    return out


def parts(value):
    high = value.astype(BF16)
    return high, (value - high.astype(F32)).astype(BF16)


def dot(a, b):
    return jnp.dot(a, b, preferred_element_type=F32)


def table_times(table_ref, value):
    high, low = parts(value)
    both = dot(table_ref[0], jnp.concatenate([high, low], 1))
    width = value.shape[1]
    return both[:, :width] + both[:, width:] + dot(table_ref[1], high)


def times_table(value, table_ref):
    high, low = parts(value)
    return dot(high, table_ref[0]) + dot(low, table_ref[0]) + dot(high, table_ref[1])


def x_first(pixels_ref, a_ref):
    @pl.loop(0, L // 8)
    def _(g):
        rows = pl.ds(pl.multiple_of(g * 8, 8), 8)
        more = pl.ds(pl.multiple_of(g * 8 + L, 8), 8)
        out = real_dft([pixels_ref[n, rows, :] for n in range(R)])
        a_ref[0, rows, :] = out[0][0]
        a_ref[0, more, :] = out[R // 2][0]
        for u in range(1, UNITS):
            a_ref[u, rows, :] = out[u][0]
            a_ref[u, more, :] = out[u][1]


def x_unit(table_ref, value):
    return table_times(table_ref, value).reshape(16, 2, 8, L)


def x_last(b_ref, out_ref):
    def body(g, top):
        rows = pl.ds(pl.multiple_of(g * 8, 8), 8)
        more = pl.ds(pl.multiple_of(g * 8 + L, 8), 8)
        z = [(b_ref[0, rows, :], None)]
        z += [(b_ref[u, rows, :], b_ref[u, more, :]) for u in range(1, UNITS)]
        z += [(b_ref[0, more, :], None)]
        out = real_dft_back(z)
        for n in range(R):
            out_ref[n, rows, :] = out[n]
        while len(out) > 1:
            out = [jnp.maximum(a, b) for a, b in zip(out[0::2], out[1::2])]
        return jnp.maximum(top, out[0])

    return lax.fori_loop(0, L // 8, body, jnp.full((8, L), -jnp.inf, F32))


def y_forward(tile_ref, twist_ref, lanes_ref, v_ref, own_ref, mirror_ref, special):
    z = complex_dft([(tile_ref[p, 0], tile_ref[p, 1]) for p in range(R)], -1)
    for a in range(R):
        re, im = z[a]
        if a:
            c, s = twist_ref[a, 0], twist_ref[a, 1]
            re, im = re * c + im * s, im * c - re * s
        v_ref[a, :, :L] = re
        v_ref[a, :, L:] = im
    own_ref[...] = times_table(v_ref[...].reshape(R * 8, 2 * L), lanes_ref).reshape(R, 8, 2 * L)

    @pl.when(special)
    def _():
        c, s = twist_ref[R, 0], twist_ref[R, 1]

        @pl.loop(0, R)
        def _(a):
            first = a == 0
            back = lax.rem(R - a, R)
            re, im = v_ref[back, :, :L], -v_ref[back, :, L:]
            mirror_ref[a, :, :L] = jnp.where(first, re, re * c + im * s)
            mirror_ref[a, :, L:] = jnp.where(first, im, im * c - re * s)

        value = mirror_ref[...].reshape(R * 8, 2 * L)
        mirror_ref[...] = times_table(value, lanes_ref).reshape(R, 8, 2 * L)


def phase(pr, pi, our, oi):
    re = pr * our + pi * oi
    im = pi * our - pr * oi
    scale = lax.rsqrt(jnp.maximum(re * re + im * im, FLOOR * FLOOR))
    return re * scale, im * scale


def y_ratio(prior_ref, own_ref, prior_mirror_ref, own_mirror_ref, v_ref, special):
    re, im = phase(prior_ref[:, :, :L], prior_ref[:, :, L:], own_ref[:, :, :L], own_ref[:, :, L:])
    v_ref[:, :, :L] = re
    v_ref[:, :, L:] = im

    @pl.when(special)
    def _():
        def both(ref, mirror, a):
            re, im, mre, mim = ref[a, :, :L], ref[a, :, L:], mirror[a, :, :L], mirror[a, :, L:]
            low = ((re + mre) * 0.5, (im + mim) * 0.5)
            high = ((im - mim) * 0.5, (mre - re) * 0.5)
            return low, high

        packed = lax.broadcasted_iota(jnp.int32, (8, L), 0) == 0

        @pl.loop(0, R)
        def _(a):
            prior_low, prior_high = both(prior_ref, prior_mirror_ref, a)
            own_low, own_high = both(own_ref, own_mirror_ref, a)
            low = phase(*prior_low, *own_low)
            high = phase(*prior_high, *own_high)
            v_ref[a, :, :L] = jnp.where(packed, low[0] - high[1], v_ref[a, :, :L])
            v_ref[a, :, L:] = jnp.where(packed, low[1] + high[0], v_ref[a, :, L:])


def y_back(v_ref, twist_ref, lanes_inv_ref, out_ref):
    v_ref[...] = times_table(v_ref[...].reshape(R * 8, 2 * L), lanes_inv_ref).reshape(R, 8, 2 * L)
    z = []
    for a in range(R):
        re, im = v_ref[a, :, :L], v_ref[a, :, L:]
        if a:
            c, s = twist_ref[a, 0], twist_ref[a, 1]
            re, im = re * c - im * s, im * c + re * s
        z.append((re, im))
    z = complex_dft(z, 1)
    for p in range(R):
        out_ref[p, 0] = z[p][0]
        out_ref[p, 1] = z[p][1]


def here():
    return lax.axis_index("section"), lax.axis_index("row")


def partners(p, step, count):
    dz = step ^ (step >> 1) ^ 2
    z = (((p >> 3) + dz) & 3) * 8
    for dy in (2, 3, 1, 0):
        y = (((p >> 1) + dy) & 3) * 2 + z
        for flip in (1, 0):
            if count:
                count -= 1
                yield y + ((p & 1) ^ flip)


def each_partner(p, act, own):
    if own:

        @pl.loop(0, 3)
        def _(step):
            for to in partners(p, step, 8):
                act(to)

        for to in partners(p, 3, 7):
            act(to)
    else:

        @pl.loop(0, 4)
        def _(step):
            for to in partners(p, step, 8):
                act(to)


def kernel(
    sec_hbm, pre_hbm, fwd_hbm, inv_hbm, twist_hbm,
    out_ref, peak_ref,
    sec_ref, pre_ref, fwd_ref, inv_ref, twist_ref,
    near_ref, a_ref, b_ref, x_ref, r_ref, y_ref, q_ref, v_ref, spec_ref, mirror_ref, mine_ref, all_ref,
    load_sem, send_sem, there_sem, back_sem, top_sem, go_sem,
):
    s, p = here()
    me = s * ROW + p
    special = me == 0
    loads = [
        pltpu.make_async_copy(source, target, load_sem.at[i])
        for i, (source, target) in enumerate(
            (
                (sec_hbm, sec_ref),
                (fwd_hbm.at[pl.ds(2 * s, 2)], near_ref),
                (pre_hbm, pre_ref),
                (fwd_hbm, fwd_ref),
                (twist_hbm.at[pl.ds(0, R + 1)], twist_ref),
                (inv_hbm, inv_ref),
            )
        )
    ]
    loads[0].start()
    loads[1].start()

    bar = pltpu.get_barrier_semaphore()

    each_partner(p, lambda to: pl.semaphore_signal(bar, inc=1, device_id=(s, to), device_id_type=MESH), True)

    def send(group, source_ref, base, target_ref, mark, sem, ready, own):
        if own:
            pltpu.make_async_copy(source_ref.at[base + p], target_ref.at[mark], ready).start()

        def one(to):
            pltpu.make_async_remote_copy(
                source_ref.at[base + to], target_ref.at[mark], sem, ready, device_id=(group, to), device_id_type=MESH
            ).start()

        each_partner(p, one, own)

    def units(group, from_ref, base, table_ref=None):
        for h in range(2):
            u = 2 * group + h
            table = fwd_ref.at[u] if table_ref is None else table_ref.at[h]
            x_ref[pl.ds(base + h * 16, 16)] = x_unit(table, from_ref[u])

    loads[0].wait()
    for load in loads[2:]:
        load.start()
    x_first(sec_ref, a_ref)
    loads[1].wait()
    units(s, a_ref, s * ROW, near_ref)

    second = (p & 1) == 1

    @pl.when(jnp.logical_not(second))
    def _():
        pl.semaphore_wait(bar, ROW - 1)
        for t in range(1, SEC):
            pl.semaphore_signal(bar, inc=1, device_id=((s + t) & (SEC - 1), p + 1), device_id_type=MESH)

    @pl.when(second)
    def _():
        pl.semaphore_wait(bar, ROW - 1 + SEC - 1)
        pl.semaphore_signal(go_sem, inc=1, device_id=(s, p - 1), device_id_type=MESH)

    send(s, x_ref, s * ROW, r_ref, me, send_sem.at[0], there_sem.at[0], True)
    loads[2].wait()
    x_first(pre_ref, b_ref)
    units(s, b_ref, DEV, near_ref)
    send(s, x_ref, DEV, r_ref, DEV + p, send_sem.at[0], there_sem.at[1], True)

    @pl.when(jnp.logical_not(second))
    def _():
        pl.semaphore_wait(go_sem, 1)

    loads[3].wait()

    def slot(t):
        group = (s + t) & (SEC - 1)
        units(group, a_ref, group * ROW)
        send(group, x_ref, group * ROW, r_ref, me, send_sem.at[0], there_sem.at[t + 1], False)

    pl.loop(1, AHEAD)(slot)

    for load in loads[4:]:
        load.wait()
    lanes_ref, lanes_inv_ref = fwd_ref.at[UNITS], inv_ref.at[UNITS]

    @pl.loop(0, SEC + 2)
    def _(k):
        @pl.when(k < SEC + 1)
        def _():
            index = jnp.where(k == 1, SEC, (s - jnp.maximum(k - 1, 0)) & (SEC - 1))
            tile = r_ref.at[pl.ds(index * ROW, ROW)]
            pltpu.make_async_copy(tile, tile, there_sem.at[k]).wait()

            @pl.when(k < SEC - AHEAD)
            def _():
                slot(k + AHEAD)

            y_forward(tile, twist_ref, lanes_ref, v_ref, spec_ref.at[index], mirror_ref.at[index], special)

        @pl.when(k >= 2)
        def _():
            own = (s - k + 2) & (SEC - 1)
            prior = jnp.where(own == 0, SEC, own - 1)
            y_ratio(spec_ref.at[prior], spec_ref.at[own], mirror_ref.at[prior], mirror_ref.at[own], v_ref, special)
            y_back(v_ref, twist_ref, lanes_inv_ref, y_ref.at[pl.ds(own * ROW, ROW)])

            @pl.when(k == 2)
            def _():
                send(s, y_ref, s * ROW, q_ref, me, send_sem.at[1], back_sem.at[0], True)

            @pl.when(k > 2)
            def _():
                send(own, y_ref, own * ROW, q_ref, me, send_sem.at[1], back_sem.at[k - 2], False)

    @pl.loop(0, SEC)
    def _(m):
        group = (s + m) & (SEC - 1)
        tile = q_ref.at[pl.ds(group * ROW, ROW)]
        pltpu.make_async_copy(tile, tile, back_sem.at[m]).wait()
        for h in range(2):
            u = 2 * group + h
            b_ref[u] = table_times(inv_ref.at[u], q_ref[pl.ds(u * 16, 16)].reshape(2 * L, L))

    top = x_last(b_ref, out_ref)

    mine_ref[...] = top
    all_ref[p] = top

    def tell(to):
        pltpu.make_async_remote_copy(
            mine_ref, all_ref.at[p], top_sem.at[0], top_sem.at[1], device_id=(s, to), device_id_type=MESH
        ).start()

    each_partner(p, tell, True)

    sent = r_ref.at[pl.ds(0, DEV + ROW - 2)]
    pltpu.make_async_copy(sent, sent, send_sem.at[0]).wait()
    sent = q_ref.at[pl.ds(0, DEV - 1)]
    pltpu.make_async_copy(sent, sent, send_sem.at[1]).wait()
    for i in range(2):
        told = all_ref.at[pl.ds(0, ROW - 1)]
        pltpu.make_async_copy(told, told, top_sem.at[i]).wait()
    peak_ref[0] = jnp.max(all_ref[...])


VMEM = pl.BlockSpec(memory_space=pltpu.VMEM)
SMEM = pl.BlockSpec(memory_space=pltpu.SMEM)
HBM = pl.BlockSpec(memory_space=pltpu.HBM)


def f32(*shape):
    return jax.ShapeDtypeStruct(shape, F32)


def local(sections, preceding):
    fwd, inv, twist = (jnp.asarray(t) for t in tables())
    args = (sections.reshape(R, L, L), preceding.reshape(R, L, L), fwd, inv, twist)
    sem = pltpu.SemaphoreType.DMA
    blocks = lambda count: pltpu.VMEM((count, 2, 8, L), F32)
    surface, peak = pl.pallas_call(
        kernel,
        out_shape=(f32(R, L, L), f32(1)),
        in_specs=[HBM] * len(args),
        out_specs=(VMEM, SMEM),
        scratch_shapes=[pltpu.VMEM(v.shape, v.dtype) for v in args[:4]]
        + [pltpu.VMEM((R + 1, 2, 8, L), F32), pltpu.VMEM((2, 2, 2 * L, 2 * L), BF16)]
        + [pltpu.VMEM((UNITS, 2 * L, L), F32)] * 2
        + [blocks(DEV + ROW), blocks(DEV + ROW), blocks(DEV), blocks(DEV)]
        + [pltpu.VMEM((R, 8, 2 * L), F32)]
        + [pltpu.VMEM((SEC + 1, R, 8, 2 * L), F32)] * 2
        + [pltpu.VMEM((8, L), F32), pltpu.VMEM((ROW, 8, L), F32)]
        + [sem((6,)), sem((2,)), sem((SEC + 1,)), sem((SEC,)), sem((2,)), pltpu.SemaphoreType.REGULAR],
        compiler_params=pltpu.CompilerParams(vmem_limit_bytes=VMEM_LIMIT, collective_id=1, has_side_effects=True),
    )(*args)
    return surface.reshape(1, N, L), peak


def solution(mesh):
    in_specs = (P("section", None, "row"), P(None, "row"))
    out_specs = (P("section", None, "row"), P("section"))
    return jax.shard_map(local, mesh=mesh, in_specs=in_specs, out_specs=out_specs, check_vma=False)
```

```python
import functools
import math

import jax
import jax.numpy as jnp
import ml_dtypes
import numpy as np
from jax import lax
from jax.experimental import pallas as pl
from jax.experimental.pallas import tpu as pltpu
from jax.sharding import PartitionSpec as P

MESH = pl.DeviceIdType.MESH
F32 = jnp.float32
BF16 = jnp.bfloat16

N = 4096
R = 32
L = 128
SEC = 8
ROW = 32
DEV = SEC * ROW
PADDED = 512
AHEAD = 3
UNITS = 16
FLOOR = 0.02 * 4096 * 4096
VMEM_LIMIT = 50 << 20


def split(table):
    high = table.astype(ml_dtypes.bfloat16)
    low = (table - high.astype(np.float64)).astype(ml_dtypes.bfloat16)
    return np.stack([high, low], -3)


@functools.lru_cache(None)
def tables():
    n2 = np.arange(L)
    row = np.arange(L)
    fwd = np.zeros((UNITS, 16, 2, 8, 2, L))
    inv = np.zeros((UNITS, 2, L, 16, 2, 8))

    def angles(kx):
        turn = 2 * np.pi / N * (np.outer(kx, n2) % N)
        return np.cos(turn).reshape(-1, 8, L), np.sin(turn).reshape(-1, 8, L)

    for u in range(1, UNITS):
        c, s = angles(u + R * row)
        fwd[u, :, 0, :, 0], fwd[u, :, 0, :, 1] = c, s
        fwd[u, :, 1, :, 0], fwd[u, :, 1, :, 1] = -s, c
        ct, st = np.moveaxis(c, 2, 0), np.moveaxis(s, 2, 0)
        inv[u, 0, :, :, 0], inv[u, 0, :, :, 1] = ct, -st
        inv[u, 1, :, :, 0], inv[u, 1, :, :, 1] = st, ct
    for half, base in ((0, 0), (1, 16)):
        c, s = angles(base + R * np.arange(L // 2))
        js = slice(8 * half, 8 * half + 8)
        ti, tr = -s, c
        bi, br = -2 * s, 2 * c
        if half == 0:
            ti[0, 0] = (-1.0) ** n2
            bi[0, 0] = (-1.0) ** n2
            br[0, 0] = 1.0
        fwd[0, js, 0, :, half], fwd[0, js, 1, :, half] = tr, ti
        inv[0, half, :, js, 0] = np.moveaxis(br, 2, 0)
        inv[0, half, :, js, 1] = np.moveaxis(bi, 2, 0)
    fwd, inv = fwd.reshape(UNITS, 2 * L, 2 * L), inv.reshape(UNITS, 2 * L, 2 * L) / N
    turn = 2 * np.pi / L * (np.outer(row, row) % L)
    c, s = np.cos(turn), np.sin(turn)
    fwd = split(np.concatenate([fwd, np.block([[c, -s], [s, c]])[None]]))
    inv = split(np.concatenate([inv, np.block([[c, s], [-s, c]])[None]]))
    turn = 2 * np.pi / N * np.outer(np.arange(R + 1), row)
    twist = np.stack([np.cos(turn), np.sin(turn)], 1).astype(np.float32)
    twist = np.broadcast_to(twist[:, :, None, :], (R + 1, 2, 8, L)).copy()
    return fwd, inv, np.pad(twist, ((0, PADDED - R - 1), (0, 0), (0, 0), (0, 0)))


def turned(z, k, n, sign):
    k %= n
    re, im = z
    if k == 0:
        return z
    if 4 * k == n:
        return (-im, re) if sign > 0 else (im, -re)
    if 2 * k == n:
        return (-re, -im)
    if 8 * k == n:
        h = math.sqrt(0.5)
        return ((re - im) * h, (re + im) * h) if sign > 0 else ((re + im) * h, (im - re) * h)
    c, s = math.cos(2 * math.pi * k / n), sign * math.sin(2 * math.pi * k / n)
    return (re * c - im * s, re * s + im * c)


def add(a, b):
    return (a[0] + b[0], a[1] + b[1])


def sub(a, b):
    return (a[0] - b[0], a[1] - b[1])


def complex_dft(z, sign):
    n = len(z)
    if n == 1:
        return z
    even, odd = complex_dft(z[0::2], sign), complex_dft(z[1::2], sign)
    out = [None] * n
    for k in range(n // 2):
        t = turned(odd[k], k, n, sign)
        out[k], out[k + n // 2] = add(even[k], t), sub(even[k], t)
    return out


def real_dft(x):
    n = len(x)
    if n == 2:
        return [(x[0] + x[1], None), (x[0] - x[1], None)]
    even, odd = real_dft(x[0::2]), real_dft(x[1::2])
    out = [None] * (n // 2 + 1)
    out[0] = (even[0][0] + odd[0][0], None)
    out[n // 2] = (even[0][0] - odd[0][0], None)
    for k in range(1, n // 4):
        t = turned(odd[k], k, n, -1)
        out[k] = add(even[k], t)
        d = sub(even[k], t)
        out[n // 2 - k] = (d[0], -d[1])
    out[n // 4] = (even[n // 4][0], -odd[n // 4][0])
    return out


def real_dft_back(z):
    n = 2 * (len(z) - 1)
    if n == 2:
        return [z[0][0] + z[1][0], z[0][0] - z[1][0]]
    even, odd = [None] * (n // 4 + 1), [None] * (n // 4 + 1)
    even[0] = (z[0][0] + z[n // 2][0], None)
    odd[0] = (z[0][0] - z[n // 2][0], None)
    for k in range(1, n // 4):
        mirror = (z[n // 2 - k][0], -z[n // 2 - k][1])
        even[k] = add(z[k], mirror)
        odd[k] = turned(sub(z[k], mirror), k, n, 1)
    even[n // 4] = (z[n // 4][0] * 2.0, None)
    odd[n // 4] = (z[n // 4][1] * -2.0, None)
    out = [None] * n
    out[0::2], out[1::2] = real_dft_back(even), real_dft_back(odd)
    return out


def parts(value):
    high = value.astype(BF16)
    return high, (value - high.astype(F32)).astype(BF16)


def dot(a, b):
    return jnp.dot(a, b, preferred_element_type=F32)


def table_times(table_ref, value):
    high, low = parts(value)
    both = dot(table_ref[0], jnp.concatenate([high, low], 1))
    width = value.shape[1]
    return both[:, :width] + both[:, width:] + dot(table_ref[1], high)


def times_table(value, table_ref):
    high, low = parts(value)
    return dot(high, table_ref[0]) + dot(low, table_ref[0]) + dot(high, table_ref[1])


def x_first(pixels_ref, a_ref):
    @pl.loop(0, L // 8)
    def _(g):
        rows = pl.ds(pl.multiple_of(g * 8, 8), 8)
        more = pl.ds(pl.multiple_of(g * 8 + L, 8), 8)
        out = real_dft([pixels_ref[n, rows, :] for n in range(R)])
        a_ref[0, rows, :] = out[0][0]
        a_ref[0, more, :] = out[R // 2][0]
        for u in range(1, UNITS):
            a_ref[u, rows, :] = out[u][0]
            a_ref[u, more, :] = out[u][1]


def x_unit(table_ref, value):
    return table_times(table_ref, value).reshape(16, 2, 8, L)


def x_last(b_ref, out_ref):
    def body(g, top):
        rows = pl.ds(pl.multiple_of(g * 8, 8), 8)
        more = pl.ds(pl.multiple_of(g * 8 + L, 8), 8)
        z = [(b_ref[0, rows, :], None)]
        z += [(b_ref[u, rows, :], b_ref[u, more, :]) for u in range(1, UNITS)]
        z += [(b_ref[0, more, :], None)]
        out = real_dft_back(z)
        for n in range(R):
            out_ref[n, rows, :] = out[n]
        while len(out) > 1:
            out = [jnp.maximum(a, b) for a, b in zip(out[0::2], out[1::2])]
        return jnp.maximum(top, out[0])

    return lax.fori_loop(0, L // 8, body, jnp.full((8, L), -jnp.inf, F32))


def y_forward(tile_ref, twist_ref, lanes_ref, v_ref, own_ref, mirror_ref, special):
    z = complex_dft([(tile_ref[p, 0], tile_ref[p, 1]) for p in range(R)], -1)
    for a in range(R):
        re, im = z[a]
        if a:
            c, s = twist_ref[a, 0], twist_ref[a, 1]
            re, im = re * c + im * s, im * c - re * s
        v_ref[a, :, :L] = re
        v_ref[a, :, L:] = im
    own_ref[...] = times_table(v_ref[...].reshape(R * 8, 2 * L), lanes_ref).reshape(R, 8, 2 * L)

    @pl.when(special)
    def _():
        c, s = twist_ref[R, 0], twist_ref[R, 1]

        @pl.loop(0, R)
        def _(a):
            first = a == 0
            back = lax.rem(R - a, R)
            re, im = v_ref[back, :, :L], -v_ref[back, :, L:]
            mirror_ref[a, :, :L] = jnp.where(first, re, re * c + im * s)
            mirror_ref[a, :, L:] = jnp.where(first, im, im * c - re * s)

        value = mirror_ref[...].reshape(R * 8, 2 * L)
        mirror_ref[...] = times_table(value, lanes_ref).reshape(R, 8, 2 * L)


def phase(pr, pi, our, oi):
    re = pr * our + pi * oi
    im = pi * our - pr * oi
    scale = lax.rsqrt(jnp.maximum(re * re + im * im, FLOOR * FLOOR))
    return re * scale, im * scale


def y_ratio(prior_ref, own_ref, prior_mirror_ref, own_mirror_ref, v_ref, special):
    re, im = phase(prior_ref[:, :, :L], prior_ref[:, :, L:], own_ref[:, :, :L], own_ref[:, :, L:])
    v_ref[:, :, :L] = re
    v_ref[:, :, L:] = im

    @pl.when(special)
    def _():
        def both(ref, mirror, a):
            re, im, mre, mim = ref[a, :, :L], ref[a, :, L:], mirror[a, :, :L], mirror[a, :, L:]
            low = ((re + mre) * 0.5, (im + mim) * 0.5)
            high = ((im - mim) * 0.5, (mre - re) * 0.5)
            return low, high

        packed = lax.broadcasted_iota(jnp.int32, (8, L), 0) == 0

        @pl.loop(0, R)
        def _(a):
            prior_low, prior_high = both(prior_ref, prior_mirror_ref, a)
            own_low, own_high = both(own_ref, own_mirror_ref, a)
            low = phase(*prior_low, *own_low)
            high = phase(*prior_high, *own_high)
            v_ref[a, :, :L] = jnp.where(packed, low[0] - high[1], v_ref[a, :, :L])
            v_ref[a, :, L:] = jnp.where(packed, low[1] + high[0], v_ref[a, :, L:])


def y_back(v_ref, twist_ref, lanes_inv_ref, out_ref):
    v_ref[...] = times_table(v_ref[...].reshape(R * 8, 2 * L), lanes_inv_ref).reshape(R, 8, 2 * L)
    z = []
    for a in range(R):
        re, im = v_ref[a, :, :L], v_ref[a, :, L:]
        if a:
            c, s = twist_ref[a, 0], twist_ref[a, 1]
            re, im = re * c - im * s, im * c + re * s
        z.append((re, im))
    z = complex_dft(z, 1)
    for p in range(R):
        out_ref[p, 0] = z[p][0]
        out_ref[p, 1] = z[p][1]


def here():
    return lax.axis_index("section"), lax.axis_index("row")


def partners(p, step, count):
    dz = step ^ (step >> 1) ^ 2
    z = (((p >> 3) + dz) & 3) * 8
    for dy in (2, 3, 1, 0):
        y = (((p >> 1) + dy) & 3) * 2 + z
        for flip in (1, 0):
            if count:
                count -= 1
                yield y + ((p & 1) ^ flip)


def each_partner(p, act, own):
    if own:

        @pl.loop(0, 3)
        def _(step):
            for to in partners(p, step, 8):
                act(to)

        for to in partners(p, 3, 7):
            act(to)
    else:

        @pl.loop(0, 4)
        def _(step):
            for to in partners(p, step, 8):
                act(to)


def kernel(
    sec_hbm, pre_hbm, fwd_hbm, inv_hbm, twist_hbm,
    out_ref, peak_ref,
    sec_ref, pre_ref, fwd_ref, inv_ref, twist_ref,
    near_ref, a_ref, b_ref, x_ref, r_ref, y_ref, q_ref, v_ref, spec_ref, mirror_ref, mine_ref, all_ref,
    load_sem, send_sem, there_sem, back_sem, top_sem, go_sem,
):
    s, p = here()
    me = s * ROW + p
    special = me == 0
    bar = pltpu.get_barrier_semaphore()

    each_partner(p, lambda to: pl.semaphore_signal(bar, inc=1, device_id=(s, to), device_id_type=MESH), True)

    loads = [
        pltpu.make_async_copy(source, target, load_sem.at[i])
        for i, (source, target) in enumerate(
            (
                (sec_hbm, sec_ref),
                (fwd_hbm.at[pl.ds(2 * s, 2)], near_ref),
                (pre_hbm, pre_ref),
                (fwd_hbm, fwd_ref),
                (twist_hbm.at[pl.ds(0, R + 1)], twist_ref),
                (inv_hbm, inv_ref),
            )
        )
    ]
    loads[0].start()
    loads[1].start()

    def send(group, source_ref, base, target_ref, mark, sem, ready, own):
        if own:
            pltpu.make_async_copy(source_ref.at[base + p], target_ref.at[mark], ready).start()

        def one(to):
            pltpu.make_async_remote_copy(
                source_ref.at[base + to], target_ref.at[mark], sem, ready, device_id=(group, to), device_id_type=MESH
            ).start()

        each_partner(p, one, own)

    def units(group, from_ref, base, table_ref=None):
        for h in range(2):
            u = 2 * group + h
            table = fwd_ref.at[u] if table_ref is None else table_ref.at[h]
            x_ref[pl.ds(base + h * 16, 16)] = x_unit(table, from_ref[u])

    loads[0].wait()
    for load in loads[2:]:
        load.start()
    x_first(sec_ref, a_ref)
    loads[1].wait()
    units(s, a_ref, s * ROW, near_ref)

    second = (p & 1) == 1

    @pl.when(jnp.logical_not(second))
    def _():
        pl.semaphore_wait(bar, ROW - 1)
        for t in range(1, SEC):
            pl.semaphore_signal(bar, inc=1, device_id=((s + t) & (SEC - 1), p + 1), device_id_type=MESH)

    @pl.when(second)
    def _():
        pl.semaphore_wait(bar, ROW - 1 + SEC - 1)
        pl.semaphore_signal(go_sem, inc=1, device_id=(s, p - 1), device_id_type=MESH)

    send(s, x_ref, s * ROW, r_ref, me, send_sem.at[0], there_sem.at[0], True)
    loads[2].wait()
    x_first(pre_ref, b_ref)
    units(s, b_ref, DEV, near_ref)
    send(s, x_ref, DEV, r_ref, DEV + p, send_sem.at[0], there_sem.at[1], True)

    @pl.when(jnp.logical_not(second))
    def _():
        pl.semaphore_wait(go_sem, 1)

    loads[3].wait()

    def slot(t):
        group = (s + t) & (SEC - 1)
        units(group, a_ref, group * ROW)
        send(group, x_ref, group * ROW, r_ref, me, send_sem.at[0], there_sem.at[t + 1], False)

    pl.loop(1, AHEAD)(slot)

    for load in loads[4:]:
        load.wait()
    lanes_ref, lanes_inv_ref = fwd_ref.at[UNITS], inv_ref.at[UNITS]

    @pl.loop(0, SEC + 2)
    def _(k):
        @pl.when(k < SEC + 1)
        def _():
            index = jnp.where(k == 1, SEC, (s - jnp.maximum(k - 1, 0)) & (SEC - 1))
            tile = r_ref.at[pl.ds(index * ROW, ROW)]
            pltpu.make_async_copy(tile, tile, there_sem.at[k]).wait()

            @pl.when(k < SEC - AHEAD)
            def _():
                slot(k + AHEAD)

            y_forward(tile, twist_ref, lanes_ref, v_ref, spec_ref.at[index], mirror_ref.at[index], special)

        @pl.when(k >= 2)
        def _():
            own = (s - k + 2) & (SEC - 1)
            prior = jnp.where(own == 0, SEC, own - 1)
            y_ratio(spec_ref.at[prior], spec_ref.at[own], mirror_ref.at[prior], mirror_ref.at[own], v_ref, special)
            y_back(v_ref, twist_ref, lanes_inv_ref, y_ref.at[pl.ds(own * ROW, ROW)])

            @pl.when(k == 2)
            def _():
                send(s, y_ref, s * ROW, q_ref, me, send_sem.at[1], back_sem.at[0], True)

            @pl.when(k > 2)
            def _():
                send(own, y_ref, own * ROW, q_ref, me, send_sem.at[1], back_sem.at[k - 2], False)

    @pl.loop(0, SEC)
    def _(m):
        group = (s + m) & (SEC - 1)
        tile = q_ref.at[pl.ds(group * ROW, ROW)]
        pltpu.make_async_copy(tile, tile, back_sem.at[m]).wait()
        for h in range(2):
            u = 2 * group + h
            b_ref[u] = table_times(inv_ref.at[u], q_ref[pl.ds(u * 16, 16)].reshape(2 * L, L))

    top = x_last(b_ref, out_ref)

    top = jnp.max(top, axis=0, keepdims=True)
    mine_ref[...] = top
    all_ref[p] = top

    def tell(to):
        pltpu.make_async_remote_copy(
            mine_ref, all_ref.at[p], top_sem.at[0], top_sem.at[1], device_id=(s, to), device_id_type=MESH
        ).start()

    each_partner(p, tell, True)

    sent = r_ref.at[pl.ds(0, DEV + ROW - 2)]
    pltpu.make_async_copy(sent, sent, send_sem.at[0]).wait()
    sent = q_ref.at[pl.ds(0, DEV - 1)]
    pltpu.make_async_copy(sent, sent, send_sem.at[1]).wait()
    for i in range(2):
        told = all_ref.at[pl.ds(0, ROW - 1)]
        pltpu.make_async_copy(told, told, top_sem.at[i]).wait()
    peak_ref[0] = jnp.max(all_ref[...])


VMEM = pl.BlockSpec(memory_space=pltpu.VMEM)
SMEM = pl.BlockSpec(memory_space=pltpu.SMEM)
HBM = pl.BlockSpec(memory_space=pltpu.HBM)


def f32(*shape):
    return jax.ShapeDtypeStruct(shape, F32)


def local(sections, preceding):
    fwd, inv, twist = (jnp.asarray(t) for t in tables())
    args = (sections.reshape(R, L, L), preceding.reshape(R, L, L), fwd, inv, twist)
    sem = pltpu.SemaphoreType.DMA
    blocks = lambda count: pltpu.VMEM((count, 2, 8, L), F32)
    surface, peak = pl.pallas_call(
        kernel,
        out_shape=(f32(R, L, L), f32(1)),
        in_specs=[HBM] * len(args),
        out_specs=(VMEM, SMEM),
        scratch_shapes=[pltpu.VMEM(v.shape, v.dtype) for v in args[:4]]
        + [pltpu.VMEM((R + 1, 2, 8, L), F32), pltpu.VMEM((2, 2, 2 * L, 2 * L), BF16)]
        + [pltpu.VMEM((UNITS, 2 * L, L), F32)] * 2
        + [blocks(DEV + ROW), blocks(DEV + ROW), blocks(DEV), blocks(DEV)]
        + [pltpu.VMEM((R, 8, 2 * L), F32)]
        + [pltpu.VMEM((SEC + 1, R, 8, 2 * L), F32)] * 2
        + [pltpu.VMEM((1, L), F32), pltpu.VMEM((ROW, 1, L), F32)]
        + [sem((6,)), sem((2,)), sem((SEC + 1,)), sem((SEC,)), sem((2,)), pltpu.SemaphoreType.REGULAR],
        compiler_params=pltpu.CompilerParams(vmem_limit_bytes=VMEM_LIMIT, collective_id=1, has_side_effects=True),
    )(*args)
    return surface.reshape(1, N, L), peak


def solution(mesh):
    in_specs = (P("section", None, "row"), P(None, "row"))
    out_specs = (P("section", None, "row"), P("section"))
    return jax.shard_map(local, mesh=mesh, in_specs=in_specs, out_specs=out_specs, check_vma=False)
```

```python
import functools
import math

import jax
import jax.numpy as jnp
import ml_dtypes
import numpy as np
from jax import lax
from jax.experimental import pallas as pl
from jax.experimental.pallas import tpu as pltpu
from jax.sharding import PartitionSpec as P

MESH = pl.DeviceIdType.MESH
F32 = jnp.float32
BF16 = jnp.bfloat16

N = 4096
R = 32
L = 128
SEC = 8
ROW = 32
DEV = SEC * ROW
PADDED = 512
AHEAD = 3
UNITS = 16
FLOOR = 0.02 * 4096 * 4096
VMEM_LIMIT = 50 << 20


def split(table):
    high = table.astype(ml_dtypes.bfloat16)
    low = (table - high.astype(np.float64)).astype(ml_dtypes.bfloat16)
    return np.stack([high, low], -3)


@functools.lru_cache(None)
def tables():
    n2 = np.arange(L)
    row = np.arange(L)
    fwd = np.zeros((UNITS, 16, 2, 8, 2, L))
    inv = np.zeros((UNITS, 2, L, 16, 2, 8))

    def angles(kx):
        turn = 2 * np.pi / N * (np.outer(kx, n2) % N)
        return np.cos(turn).reshape(-1, 8, L), np.sin(turn).reshape(-1, 8, L)

    for u in range(1, UNITS):
        c, s = angles(u + R * row)
        fwd[u, :, 0, :, 0], fwd[u, :, 0, :, 1] = c, s
        fwd[u, :, 1, :, 0], fwd[u, :, 1, :, 1] = -s, c
        ct, st = np.moveaxis(c, 2, 0), np.moveaxis(s, 2, 0)
        inv[u, 0, :, :, 0], inv[u, 0, :, :, 1] = ct, -st
        inv[u, 1, :, :, 0], inv[u, 1, :, :, 1] = st, ct
    for half, base in ((0, 0), (1, 16)):
        c, s = angles(base + R * np.arange(L // 2))
        js = slice(8 * half, 8 * half + 8)
        ti, tr = -s, c
        bi, br = -2 * s, 2 * c
        if half == 0:
            ti[0, 0] = (-1.0) ** n2
            bi[0, 0] = (-1.0) ** n2
            br[0, 0] = 1.0
        fwd[0, js, 0, :, half], fwd[0, js, 1, :, half] = tr, ti
        inv[0, half, :, js, 0] = np.moveaxis(br, 2, 0)
        inv[0, half, :, js, 1] = np.moveaxis(bi, 2, 0)
    fwd, inv = fwd.reshape(UNITS, 2 * L, 2 * L), inv.reshape(UNITS, 2 * L, 2 * L) / N
    turn = 2 * np.pi / L * (np.outer(row, row) % L)
    c, s = np.cos(turn), np.sin(turn)
    fwd = split(np.concatenate([fwd, np.block([[c, -s], [s, c]])[None]]))
    inv = split(np.concatenate([inv, np.block([[c, s], [-s, c]])[None]]))
    turn = 2 * np.pi / N * np.outer(np.arange(R + 1), row)
    twist = np.stack([np.cos(turn), np.sin(turn)], 1).astype(np.float32)
    twist = np.broadcast_to(twist[:, :, None, :], (R + 1, 2, 8, L)).copy()
    return fwd, inv, np.pad(twist, ((0, PADDED - R - 1), (0, 0), (0, 0), (0, 0)))


def turned(z, k, n, sign):
    k %= n
    re, im = z
    if k == 0:
        return z
    if 4 * k == n:
        return (-im, re) if sign > 0 else (im, -re)
    if 2 * k == n:
        return (-re, -im)
    if 8 * k == n:
        h = math.sqrt(0.5)
        return ((re - im) * h, (re + im) * h) if sign > 0 else ((re + im) * h, (im - re) * h)
    c, s = math.cos(2 * math.pi * k / n), sign * math.sin(2 * math.pi * k / n)
    return (re * c - im * s, re * s + im * c)


def add(a, b):
    return (a[0] + b[0], a[1] + b[1])


def sub(a, b):
    return (a[0] - b[0], a[1] - b[1])


def complex_dft(z, sign):
    n = len(z)
    if n == 1:
        return z
    even, odd = complex_dft(z[0::2], sign), complex_dft(z[1::2], sign)
    out = [None] * n
    for k in range(n // 2):
        t = turned(odd[k], k, n, sign)
        out[k], out[k + n // 2] = add(even[k], t), sub(even[k], t)
    return out


def real_dft(x):
    n = len(x)
    if n == 2:
        return [(x[0] + x[1], None), (x[0] - x[1], None)]
    even, odd = real_dft(x[0::2]), real_dft(x[1::2])
    out = [None] * (n // 2 + 1)
    out[0] = (even[0][0] + odd[0][0], None)
    out[n // 2] = (even[0][0] - odd[0][0], None)
    for k in range(1, n // 4):
        t = turned(odd[k], k, n, -1)
        out[k] = add(even[k], t)
        d = sub(even[k], t)
        out[n // 2 - k] = (d[0], -d[1])
    out[n // 4] = (even[n // 4][0], -odd[n // 4][0])
    return out


def real_dft_back(z):
    n = 2 * (len(z) - 1)
    if n == 2:
        return [z[0][0] + z[1][0], z[0][0] - z[1][0]]
    even, odd = [None] * (n // 4 + 1), [None] * (n // 4 + 1)
    even[0] = (z[0][0] + z[n // 2][0], None)
    odd[0] = (z[0][0] - z[n // 2][0], None)
    for k in range(1, n // 4):
        mirror = (z[n // 2 - k][0], -z[n // 2 - k][1])
        even[k] = add(z[k], mirror)
        odd[k] = turned(sub(z[k], mirror), k, n, 1)
    even[n // 4] = (z[n // 4][0] * 2.0, None)
    odd[n // 4] = (z[n // 4][1] * -2.0, None)
    out = [None] * n
    out[0::2], out[1::2] = real_dft_back(even), real_dft_back(odd)
    return out


def parts(value):
    high = value.astype(BF16)
    return high, (value - high.astype(F32)).astype(BF16)


def dot(a, b):
    return jnp.dot(a, b, preferred_element_type=F32)


def table_times(table_ref, value):
    high, low = parts(value)
    both = dot(table_ref[0], jnp.concatenate([high, low], 1))
    width = value.shape[1]
    return both[:, :width] + both[:, width:] + dot(table_ref[1], high)


def times_table(value, table_ref):
    high, low = parts(value)
    return dot(high, table_ref[0]) + dot(low, table_ref[0]) + dot(high, table_ref[1])


def x_first(pixels_ref, a_ref):
    @pl.loop(0, L // 8)
    def _(g):
        rows = pl.ds(pl.multiple_of(g * 8, 8), 8)
        more = pl.ds(pl.multiple_of(g * 8 + L, 8), 8)
        out = real_dft([pixels_ref[n, rows, :] for n in range(R)])
        a_ref[0, rows, :] = out[0][0]
        a_ref[0, more, :] = out[R // 2][0]
        for u in range(1, UNITS):
            a_ref[u, rows, :] = out[u][0]
            a_ref[u, more, :] = out[u][1]


def x_unit(table_ref, value):
    return table_times(table_ref, value).reshape(16, 2, 8, L)


def x_last(b_ref, out_ref):
    def body(g, top):
        rows = pl.ds(pl.multiple_of(g * 8, 8), 8)
        more = pl.ds(pl.multiple_of(g * 8 + L, 8), 8)
        z = [(b_ref[0, rows, :], None)]
        z += [(b_ref[u, rows, :], b_ref[u, more, :]) for u in range(1, UNITS)]
        z += [(b_ref[0, more, :], None)]
        out = real_dft_back(z)
        for n in range(R):
            out_ref[n, rows, :] = out[n]
        while len(out) > 1:
            out = [jnp.maximum(a, b) for a, b in zip(out[0::2], out[1::2])]
        return jnp.maximum(top, out[0])

    return lax.fori_loop(0, L // 8, body, jnp.full((8, L), -jnp.inf, F32), unroll=2)


def y_forward(tile_ref, twist_ref, lanes_ref, v_ref, own_ref, mirror_ref, special):
    z = complex_dft([(tile_ref[p, 0], tile_ref[p, 1]) for p in range(R)], -1)
    for a in range(R):
        re, im = z[a]
        if a:
            c, s = twist_ref[a, 0], twist_ref[a, 1]
            re, im = re * c + im * s, im * c - re * s
        v_ref[a, :, :L] = re
        v_ref[a, :, L:] = im
    own_ref[...] = times_table(v_ref[...].reshape(R * 8, 2 * L), lanes_ref).reshape(R, 8, 2 * L)

    @pl.when(special)
    def _():
        c, s = twist_ref[R, 0], twist_ref[R, 1]

        @pl.loop(0, R)
        def _(a):
            first = a == 0
            back = lax.rem(R - a, R)
            re, im = v_ref[back, :, :L], -v_ref[back, :, L:]
            mirror_ref[a, :, :L] = jnp.where(first, re, re * c + im * s)
            mirror_ref[a, :, L:] = jnp.where(first, im, im * c - re * s)

        value = mirror_ref[...].reshape(R * 8, 2 * L)
        mirror_ref[...] = times_table(value, lanes_ref).reshape(R, 8, 2 * L)


def phase(pr, pi, our, oi):
    re = pr * our + pi * oi
    im = pi * our - pr * oi
    scale = lax.rsqrt(jnp.maximum(re * re + im * im, FLOOR * FLOOR))
    return re * scale, im * scale


def y_ratio(prior_ref, own_ref, prior_mirror_ref, own_mirror_ref, v_ref, special):
    re, im = phase(prior_ref[:, :, :L], prior_ref[:, :, L:], own_ref[:, :, :L], own_ref[:, :, L:])
    v_ref[:, :, :L] = re
    v_ref[:, :, L:] = im

    @pl.when(special)
    def _():
        def both(ref, mirror, a):
            re, im, mre, mim = ref[a, :, :L], ref[a, :, L:], mirror[a, :, :L], mirror[a, :, L:]
            low = ((re + mre) * 0.5, (im + mim) * 0.5)
            high = ((im - mim) * 0.5, (mre - re) * 0.5)
            return low, high

        packed = lax.broadcasted_iota(jnp.int32, (8, L), 0) == 0

        @pl.loop(0, R)
        def _(a):
            prior_low, prior_high = both(prior_ref, prior_mirror_ref, a)
            own_low, own_high = both(own_ref, own_mirror_ref, a)
            low = phase(*prior_low, *own_low)
            high = phase(*prior_high, *own_high)
            v_ref[a, :, :L] = jnp.where(packed, low[0] - high[1], v_ref[a, :, :L])
            v_ref[a, :, L:] = jnp.where(packed, low[1] + high[0], v_ref[a, :, L:])


def y_back(v_ref, twist_ref, lanes_inv_ref, out_ref):
    v_ref[...] = times_table(v_ref[...].reshape(R * 8, 2 * L), lanes_inv_ref).reshape(R, 8, 2 * L)
    z = []
    for a in range(R):
        re, im = v_ref[a, :, :L], v_ref[a, :, L:]
        if a:
            c, s = twist_ref[a, 0], twist_ref[a, 1]
            re, im = re * c - im * s, im * c + re * s
        z.append((re, im))
    z = complex_dft(z, 1)
    for p in range(R):
        out_ref[p, 0] = z[p][0]
        out_ref[p, 1] = z[p][1]


def here():
    return lax.axis_index("section"), lax.axis_index("row")


def partners(p, step, count):
    dz = step ^ (step >> 1) ^ 2
    z = (((p >> 3) + dz) & 3) * 8
    for dy in (2, 3, 1, 0):
        y = (((p >> 1) + dy) & 3) * 2 + z
        for flip in (1, 0):
            if count:
                count -= 1
                yield y + ((p & 1) ^ flip)


def each_partner(p, act, own):
    if own:

        @pl.loop(0, 3)
        def _(step):
            for to in partners(p, step, 8):
                act(to)

        for to in partners(p, 3, 7):
            act(to)
    else:

        @pl.loop(0, 4)
        def _(step):
            for to in partners(p, step, 8):
                act(to)


def kernel(
    sec_hbm, pre_hbm, fwd_hbm, inv_hbm, twist_hbm,
    out_ref, peak_ref,
    sec_ref, pre_ref, fwd_ref, inv_ref, twist_ref,
    near_ref, a_ref, b_ref, x_ref, r_ref, y_ref, q_ref, v_ref, spec_ref, mirror_ref, mine_ref, all_ref,
    load_sem, send_sem, there_sem, back_sem, top_sem, go_sem,
):
    s, p = here()
    me = s * ROW + p
    special = me == 0
    bar = pltpu.get_barrier_semaphore()

    each_partner(p, lambda to: pl.semaphore_signal(bar, inc=1, device_id=(s, to), device_id_type=MESH), True)

    loads = [
        pltpu.make_async_copy(source, target, load_sem.at[i])
        for i, (source, target) in enumerate(
            (
                (sec_hbm, sec_ref),
                (fwd_hbm.at[pl.ds(2 * s, 2)], near_ref),
                (pre_hbm, pre_ref),
                (fwd_hbm, fwd_ref),
                (twist_hbm.at[pl.ds(0, R + 1)], twist_ref),
                (inv_hbm, inv_ref),
            )
        )
    ]
    loads[0].start()
    loads[1].start()

    def send(group, source_ref, base, target_ref, mark, sem, ready, own):
        if own:
            pltpu.make_async_copy(source_ref.at[base + p], target_ref.at[mark], ready).start()

        def one(to):
            pltpu.make_async_remote_copy(
                source_ref.at[base + to], target_ref.at[mark], sem, ready, device_id=(group, to), device_id_type=MESH
            ).start()

        each_partner(p, one, own)

    def units(group, from_ref, base, table_ref=None):
        for h in range(2):
            u = 2 * group + h
            table = fwd_ref.at[u] if table_ref is None else table_ref.at[h]
            x_ref[pl.ds(base + h * 16, 16)] = x_unit(table, from_ref[u])

    loads[0].wait()
    for load in loads[2:]:
        load.start()
    x_first(sec_ref, a_ref)
    loads[1].wait()
    units(s, a_ref, s * ROW, near_ref)

    second = (p & 1) == 1

    @pl.when(jnp.logical_not(second))
    def _():
        pl.semaphore_wait(bar, ROW - 1)
        for t in range(1, SEC):
            pl.semaphore_signal(bar, inc=1, device_id=((s + t) & (SEC - 1), p + 1), device_id_type=MESH)

    @pl.when(second)
    def _():
        pl.semaphore_wait(bar, ROW - 1 + SEC - 1)
        pl.semaphore_signal(go_sem, inc=1, device_id=(s, p - 1), device_id_type=MESH)

    send(s, x_ref, s * ROW, r_ref, me, send_sem.at[0], there_sem.at[0], True)
    loads[2].wait()
    x_first(pre_ref, b_ref)
    units(s, b_ref, DEV, near_ref)
    send(s, x_ref, DEV, r_ref, DEV + p, send_sem.at[0], there_sem.at[1], True)

    @pl.when(jnp.logical_not(second))
    def _():
        pl.semaphore_wait(go_sem, 1)

    loads[3].wait()

    def slot(t):
        group = (s + t) & (SEC - 1)
        units(group, a_ref, group * ROW)
        send(group, x_ref, group * ROW, r_ref, me, send_sem.at[0], there_sem.at[t + 1], False)

    pl.loop(1, AHEAD)(slot)

    for load in loads[4:]:
        load.wait()
    lanes_ref, lanes_inv_ref = fwd_ref.at[UNITS], inv_ref.at[UNITS]

    @pl.loop(0, SEC + 2)
    def _(k):
        @pl.when(k < SEC + 1)
        def _():
            index = jnp.where(k == 1, SEC, (s - jnp.maximum(k - 1, 0)) & (SEC - 1))
            tile = r_ref.at[pl.ds(index * ROW, ROW)]
            pltpu.make_async_copy(tile, tile, there_sem.at[k]).wait()

            @pl.when(k < SEC - AHEAD)
            def _():
                slot(k + AHEAD)

            y_forward(tile, twist_ref, lanes_ref, v_ref, spec_ref.at[index], mirror_ref.at[index], special)

        @pl.when(k >= 2)
        def _():
            own = (s - k + 2) & (SEC - 1)
            prior = jnp.where(own == 0, SEC, own - 1)
            y_ratio(spec_ref.at[prior], spec_ref.at[own], mirror_ref.at[prior], mirror_ref.at[own], v_ref, special)
            y_back(v_ref, twist_ref, lanes_inv_ref, y_ref.at[pl.ds(own * ROW, ROW)])

            @pl.when(k == 2)
            def _():
                send(s, y_ref, s * ROW, q_ref, me, send_sem.at[1], back_sem.at[0], True)

            @pl.when(k > 2)
            def _():
                send(own, y_ref, own * ROW, q_ref, me, send_sem.at[1], back_sem.at[k - 2], False)

    @pl.loop(0, SEC)
    def _(m):
        group = (s + m) & (SEC - 1)
        tile = q_ref.at[pl.ds(group * ROW, ROW)]
        pltpu.make_async_copy(tile, tile, back_sem.at[m]).wait()
        for h in range(2):
            u = 2 * group + h
            b_ref[u] = table_times(inv_ref.at[u], q_ref[pl.ds(u * 16, 16)].reshape(2 * L, L))

    top = x_last(b_ref, out_ref)

    top = jnp.max(top, axis=0, keepdims=True)
    mine_ref[...] = top
    all_ref[p] = top

    def tell(to):
        pltpu.make_async_remote_copy(
            mine_ref, all_ref.at[p], top_sem.at[0], top_sem.at[1], device_id=(s, to), device_id_type=MESH
        ).start()

    each_partner(p, tell, True)

    sent = r_ref.at[pl.ds(0, DEV + ROW - 2)]
    pltpu.make_async_copy(sent, sent, send_sem.at[0]).wait()
    sent = q_ref.at[pl.ds(0, DEV - 1)]
    pltpu.make_async_copy(sent, sent, send_sem.at[1]).wait()
    for i in range(2):
        told = all_ref.at[pl.ds(0, ROW - 1)]
        pltpu.make_async_copy(told, told, top_sem.at[i]).wait()
    peak_ref[0] = jnp.max(all_ref[...])


VMEM = pl.BlockSpec(memory_space=pltpu.VMEM)
SMEM = pl.BlockSpec(memory_space=pltpu.SMEM)
HBM = pl.BlockSpec(memory_space=pltpu.HBM)


def f32(*shape):
    return jax.ShapeDtypeStruct(shape, F32)


def local(sections, preceding):
    fwd, inv, twist = (jnp.asarray(t) for t in tables())
    args = (sections.reshape(R, L, L), preceding.reshape(R, L, L), fwd, inv, twist)
    sem = pltpu.SemaphoreType.DMA
    blocks = lambda count: pltpu.VMEM((count, 2, 8, L), F32)
    surface, peak = pl.pallas_call(
        kernel,
        out_shape=(f32(R, L, L), f32(1)),
        in_specs=[HBM] * len(args),
        out_specs=(VMEM, SMEM),
        scratch_shapes=[pltpu.VMEM(v.shape, v.dtype) for v in args[:4]]
        + [pltpu.VMEM((R + 1, 2, 8, L), F32), pltpu.VMEM((2, 2, 2 * L, 2 * L), BF16)]
        + [pltpu.VMEM((UNITS, 2 * L, L), F32)] * 2
        + [blocks(DEV + ROW), blocks(DEV + ROW), blocks(DEV), blocks(DEV)]
        + [pltpu.VMEM((R, 8, 2 * L), F32)]
        + [pltpu.VMEM((SEC + 1, R, 8, 2 * L), F32)] * 2
        + [pltpu.VMEM((1, L), F32), pltpu.VMEM((ROW, 1, L), F32)]
        + [sem((6,)), sem((2,)), sem((SEC + 1,)), sem((SEC,)), sem((2,)), pltpu.SemaphoreType.REGULAR],
        compiler_params=pltpu.CompilerParams(vmem_limit_bytes=VMEM_LIMIT, collective_id=1, has_side_effects=True),
    )(*args)
    return surface.reshape(1, N, L), peak


def solution(mesh):
    in_specs = (P("section", None, "row"), P(None, "row"))
    out_specs = (P("section", None, "row"), P("section"))
    return jax.shard_map(local, mesh=mesh, in_specs=in_specs, out_specs=out_specs, check_vma=False)
```
